512 devices in a mesh: space: 128 (over z, y, core), rhs: 4 (over x).
Axes of the slice: x: 4, y: 8, z: 8, core: 2. Of those that a mesh axis runs over, the one named last changes fastest.
Arguments:
- right_sides: bfloat16 [4096, 128, 128], P('space', 'rhs'), may hold values from -6 to 6
- off_blocks: bfloat16 [4096, 5, 128, 128], P('space'), may hold values from -0.1875 to 0.1875
- diag_inv: bfloat16 [4096, 128, 128], P('space')
- neighbors: int32 [4096, 5], P('space'), may hold values from 0 to 4095, as said below
- level_of: int32 [4096], replicated, may hold values from 0 to 3, as said below
Outputs:
- solution: bfloat16 [4096, 128, 128], P('space', 'rhs')
The draws below stay inside these ranges and needn't reach their ends.
Inputs may be any that keep to these rules, and one draw needn't show every extreme that they name: `level_of`: in each device's 32 block rows no level holds more than 16 rows, and some level holds exactly 16. `neighbors`: each block column lies among the rows of the devices at most 2 indices away along space from the row's own device, and that distance 2 is reached.
All inputs are finite; a program needn't handle non-finite values.
Results may differ from the reference program's by a relative error of at most 0.0058.
Values may be sent and summed in bfloat16 or wider, within the bound.
A program may use at most 64 MiB of HBM per device.

```python
import math
import jax
import jax.numpy as jnp

BLK = 128
RHS = 128
NEIGH = 5
LEVELS = 4
REACH = 2
ROWS_DEV = 32
CAP = 16
NROWS = 4096


def draw_diag_inv(key, part):
    key = jax.random.fold_in(key, 7)
    key_scale, key_noise = jax.random.split(key)
    scales = jax.random.uniform(key_scale, (NROWS, BLK), minval=0.6, maxval=1.4)
    noise = jax.random.normal(key_noise, (NROWS, BLK, BLK)) * (0.45 / math.sqrt(BLK))
    identity = jnp.eye(BLK, dtype=jnp.float32)
    return (identity[None] * scales[:, :, None] + noise).astype(jnp.bfloat16)


def draw_neighbors(key, part):
    key = jax.random.fold_in(key, 5)
    key_offset, key_inner = jax.random.split(key)
    groups = NROWS // ROWS_DEV
    rows = jnp.arange(NROWS, dtype=jnp.int32)
    owner = rows // ROWS_DEV
    position = rows % ROWS_DEV
    slot = jnp.arange(NEIGH, dtype=jnp.int32)[None, :]
    offsets = jax.random.randint(key_offset, (NROWS, NEIGH), -REACH, REACH + 1)
    offsets = jnp.where(slot == 0, -REACH, jnp.where(slot == 1, REACH, offsets))
    target = jnp.clip(owner[:, None] + offsets, 0, groups - 1)
    inner = jax.random.randint(key_inner, (NROWS, NEIGH), 0, ROWS_DEV)
    inner = jnp.where(slot < 2, position[:, None], inner)
    return (target * ROWS_DEV + inner).astype(jnp.int32)


def draw_level_of(key, part):
    key = jax.random.fold_in(key, 11)
    key_label, key_place = jax.random.split(key)
    positions = jnp.arange(ROWS_DEV)
    base_levels = jnp.where(positions < CAP, 0, (positions - CAP) % (LEVELS - 1) + 1)
    groups = NROWS // ROWS_DEV
    labels = jax.vmap(lambda k: jax.random.permutation(k, LEVELS))(jax.random.split(key_label, groups))
    named = jnp.take_along_axis(labels, jnp.broadcast_to(base_levels[None, :], (groups, ROWS_DEV)), axis=1)
    shuffles = jax.vmap(lambda k: jax.random.permutation(k, ROWS_DEV))(jax.random.split(key_place, groups))
    placed = jnp.take_along_axis(named, shuffles, axis=1)
    return placed.reshape(-1).astype(jnp.int32)


def steps_of(key, shape, cuts, smallest, largest):
    gain, own = 1.0, jax.random.fold_in(key, 6)
    for dim, blocks in cuts:
        heights = jnp.exp(jax.random.uniform(jax.random.fold_in(own, dim), (blocks,), jnp.float32, smallest / len(cuts), largest / len(cuts)))
        gain = gain * jnp.repeat(heights, shape[dim] // blocks).reshape([-1 if axis == dim else 1 for axis in range(len(shape))])
    return gain


def centred(rng, extent, scale, reach, cuts=(), kind=jnp.bfloat16):
    array = scale * jax.random.normal(rng, extent, jnp.float32)
    if cuts:
        array = array * steps_of(rng, extent, cuts, -0.22, 0.18)
    return jnp.clip(array, -reach, reach).astype(kind)


def setup_inputs(seed: int = 0) -> dict:
    seeds = jax.random.split(jax.random.key(seed), 6)
    right_sides = centred(seeds[0], (NROWS, RHS, BLK), 1.0, 6.0, ((0, 128), (1, 4)))
    off_blocks = centred(seeds[1], (NROWS, NEIGH, BLK, BLK), (8 * BLK) ** -0.5, 0.1875, ((0, 128),))
    diag_inv = draw_diag_inv(jax.random.fold_in(seeds[5], 71), 0)
    neighbors = draw_neighbors(jax.random.fold_in(seeds[5], 71), 0)
    level_of = draw_level_of(jax.random.fold_in(seeds[5], 71), 0)
    return dict(right_sides=right_sides, off_blocks=off_blocks, diag_inv=diag_inv, neighbors=neighbors, level_of=level_of)


def reference(right_sides, off_blocks, diag_inv, neighbors, level_of):
    their_level = level_of[neighbors]
    lower = (their_level < level_of[:, None]).astype(jnp.int32)
    upper = (their_level > level_of[:, None]).astype(jnp.int32)
    blocks_wide = off_blocks.astype(jnp.float32)

    def apply_terms(values, chosen):
        picked = values[neighbors].astype(jnp.float32) * chosen[:, :, None, None].astype(jnp.float32)
        return jnp.einsum('rkab,rkjb->rja', blocks_wide, picked)

    forward = jnp.zeros(right_sides.shape, jnp.bfloat16)
    for level_now in range(LEVELS):
        new_rows = (right_sides.astype(jnp.float32) - apply_terms(forward, lower)).astype(jnp.bfloat16)
        forward = jnp.where((level_of == level_now)[:, None, None], new_rows, forward)
    solution = jnp.zeros(right_sides.shape, jnp.bfloat16)
    inverse_wide = diag_inv.astype(jnp.float32)
    for level_now in reversed(range(LEVELS)):
        reduced = (forward.astype(jnp.float32) - apply_terms(solution, upper)).astype(jnp.bfloat16)
        new_rows = jnp.einsum('rab,rjb->rja', inverse_wide, reduced.astype(jnp.float32)).astype(jnp.bfloat16)
        solution = jnp.where((level_of == level_now)[:, None, None], new_rows, solution)
    return solution
```

```python
import functools

import jax
import jax.numpy as jnp
from jax import lax
from jax.experimental import pallas as pl
from jax.experimental.pallas import tpu as pltpu
from jax.sharding import PartitionSpec as P

MESH = pl.DeviceIdType.MESH
LEVELS = 4
REACH = 2
NEIGH = 5
CAP = 16
STEPS = 6
CHUNK = 4
PIECES = CAP // CHUNK
SIBLING, NEAR, FAR, PASSED, OWN = range(5)
SPAN = 5 * CAP
ZERO = STEPS * SPAN
ROW, PLACE = NEIGH, NEIGH + 1


def window(me, count, level_ref, rows):
    per_line = 128 // rows
    across = lax.broadcasted_iota(jnp.int32, (rows, rows), 1)
    down = lax.broadcasted_iota(jnp.int32, (rows, rows), 0)

    def stand(row):
        return jnp.sum(jnp.where(across == down, row, 0), axis=1, keepdims=True)

    def levels(offset):
        device = jnp.clip(me + offset, 0, count - 1)
        line = level_ref[pl.ds(device // per_line, 1), :]
        part = device % per_line
        here = jnp.zeros((1, rows), jnp.int32)
        for t in range(per_line):
            here = jnp.where(part == t, line[:, t * rows : (t + 1) * rows], here)
        here = jnp.broadcast_to(here, (rows, rows))
        return here, stand(here)

    def ranks(here, column):
        earlier = jnp.where((column == here) & (down < across), 1, 0)
        return jnp.minimum(jnp.sum(earlier, axis=0, keepdims=True), CAP - 1)

    return across, down, stand, levels, ranks


def columns():
    lane = lax.broadcasted_iota(jnp.int32, (1, 128), 1)
    number = lane // CAP
    return lane, number, jnp.where(number < 3, number + 1, 5 - number)


def fill_rows(me, count, level_ref, rows, table_ref):
    across, down, _, levels, ranks = window(me, count, level_ref, rows)
    here, column = levels(0)
    earlier = jnp.where((column == here) & (across < down), 1, 0)
    slot = column * CAP + jnp.sum(earlier, axis=1, keepdims=True)
    lane, _, solves = columns()
    place = slot == jnp.broadcast_to(solves * CAP + lane % CAP, (rows, 128))
    number = lax.broadcasted_iota(jnp.int32, (rows, 128), 0)
    row_of = jnp.sum(jnp.where(place, number, 0), axis=0, keepdims=True)
    table_ref[ROW : ROW + 1, :] = jnp.clip(row_of, 0, rows - 1)
    table_ref[PLACE : PLACE + 1, 0:rows] = jnp.clip(here[0:1, :] * CAP + ranks(here, column), 0, LEVELS * CAP - 1)
    return place


def fill_terms(me, parity, count, level_ref, neighbor_ref, rows, place, table_ref):
    across, _, stand, levels, ranks = window(me, count, level_ref, rows)
    _, number, solves = columns()
    sections = {-2: FAR - parity, -1: PASSED - 3 * parity, 0: OWN, 1: 3 * parity, 2: NEAR + parity}
    codes = []
    for offset in range(-REACH, REACH + 1):
        here, column = levels(offset)
        codes.append(here * 128 + ranks(here, column) + sections[offset] * CAP)
    for k in range(NEIGH):
        row = jnp.broadcast_to(neighbor_ref[k : k + 1, :], (rows, rows))
        which = stand(row) - (me - REACH) * rows
        found = jnp.zeros((rows, rows), jnp.int32)
        for j in range(2 * REACH + 1):
            found += jnp.where(which - j * rows == across, codes[j], 0)
        code = jnp.sum(found, axis=1, keepdims=True)
        by_slot = jnp.sum(jnp.where(place, code, 0), axis=0, keepdims=True)
        spot, level = by_slot & 127, by_slot >> 7
        lower = (number < 3) & (level < solves)
        upper = (number >= 3) & (level > solves)
        index = jnp.where(lower, level * SPAN + spot, jnp.where(upper, (STEPS - level) * SPAN + spot, ZERO))
        table_ref[k : k + 1, :] = jnp.clip(index, 0, ZERO)


def kernel(count, level_ref, neighbor_ref, right_hbm, off_hbm, inverse_hbm, out_ref,
           right, off, inverse, table_v, table, value, solved, leaving, arriving,
           load_sem, send_sem, near_sem, other_sem):
    me = lax.axis_index("space")
    parity = lax.rem(me, 2)
    sibling = me + 1 - 2 * parity
    to_near, to_far = me - 2 + 4 * parity, me + 2 - 4 * parity
    has_near = (to_near >= 0) & (to_near < count)
    has_far = (to_far >= 0) & (to_far < count)

    barrier = pltpu.get_barrier_semaphore()

    def greet(*targets):
        for target in targets:
            pl.semaphore_signal(barrier, inc=1, device_id={"space": target}, device_id_type=MESH)

    greet(sibling)
    pl.when(has_near)(lambda: greet(to_near))
    pl.when(has_far)(lambda: greet(to_far))

    rows = right.shape[0]
    load_right = pltpu.make_async_copy(right_hbm, right, load_sem.at[0])
    load_right.start()
    for start in range(0, rows, 4):
        part = pl.ds(start, 4)
        pltpu.make_async_copy(off_hbm.at[part], off.at[part], load_sem.at[1]).start()
    load_off = pltpu.make_async_copy(off_hbm, off, load_sem.at[1])
    load_inverse = pltpu.make_async_copy(inverse_hbm, inverse, load_sem.at[2])
    load_inverse.start()
    load_table = pltpu.make_async_copy(table_v, table, load_sem.at[3])

    table_v[...] = jnp.zeros_like(table_v)
    place = fill_rows(me, count, level_ref, rows, table_v)
    load_table.start()
    solved[ZERO] = jnp.zeros(solved.shape[1:], solved.dtype)

    def remote(source, target, kind, step, to, sem):
        return pltpu.make_async_remote_copy(
            src_ref=source, dst_ref=target, send_sem=send_sem.at[kind, step], recv_sem=sem,
            device_id={"space": to}, device_id_type=MESH,
        )

    def section(step, which, start=0, size=CAP):
        return arriving.at[step, pl.ds(which * CAP + start, size)]

    def own(step, start=0, size=CAP):
        return leaving.at[step, pl.ds(start, size)]

    def send_near(step, piece):
        at = piece * CHUNK

        @pl.when(has_near)
        def _():
            remote(own(step, at, CHUNK), section(step, NEAR, at, CHUNK), 1, step, to_near,
                   near_sem.at[step, piece]).start()

    def send_far(step, start, size):
        @pl.when(has_far)
        def _():
            remote(own(step, start, size), section(step, FAR, start, size), 2, step, to_far,
                   other_sem.at[step, 1]).start()

    def send_sibling(step):
        remote(own(step), section(step, SIBLING), 0, step, sibling, other_sem.at[step, 0]).start()

    def arrived(step, which, start, size, sem):
        there = section(step, which, start, size)
        remote(there, there, 0, step, sibling, sem).wait_recv()

    def keep(step, which):
        solved[pl.ds(step * SPAN + which * CAP, CAP)] = arriving[step, pl.ds(which * CAP, CAP)]

    def receive(step):
        @pl.when(has_far)
        def _():
            for piece in range(PIECES):
                at = piece * CHUNK
                arrived(step, NEAR, at, CHUNK, near_sem.at[step, piece])
                remote(section(step, NEAR, at, CHUNK), section(step, PASSED, at, CHUNK), 3, step, sibling,
                       other_sem.at[step, 2]).start()
            keep(step, NEAR)

        arrived(step, SIBLING, 0, CAP, other_sem.at[step, 0])
        keep(step, SIBLING)

        @pl.when(has_near)
        def _():
            arrived(step, FAR, 0, CAP, other_sem.at[step, 1])
            keep(step, FAR)
            arrived(step, PASSED, 0, CAP, other_sem.at[step, 2])
            keep(step, PASSED)

    def paired(lefts, blocks):
        both = lax.dot_general(
            jnp.concatenate(lefts, axis=0), jnp.concatenate(blocks, axis=0),
            (((1,), (1,)), ((), ())), preferred_element_type=jnp.float32,
        )
        height, width = lefts[0].shape[0], blocks[0].shape[0]
        return both[:height, :width], both[height:, width:]

    def solve(step, level, inverted):
        def pair(s):
            ats = [(step - 1) * CAP + s + t for t in range(2)]
            two = [table[ROW, at] for at in ats]
            lefts = [jnp.concatenate([solved[table[k, at]] for k in range(NEIGH)], axis=1) for at in ats]
            blocks = [jnp.concatenate([off[row, k] for k in range(NEIGH)], axis=1) for row in two]
            news = [
                (value[level * CAP + s + t].astype(jnp.float32) - total).astype(jnp.bfloat16)
                for t, total in enumerate(paired(lefts, blocks))
            ]
            if inverted:
                news = [new.astype(jnp.bfloat16) for new in paired(news, [inverse[row] for row in two])]
            return news

        def send(piece, last):
            send_near(step, piece)
            if last:
                send_far(step, (piece - 1) * CHUNK, 2 * CHUNK)

        def half(h, _):
            for p in range(PIECES // 2):
                piece = h * (PIECES // 2) + p
                news = sum([pair(piece * CHUNK + t) for t in range(0, CHUNK, 2)], [])
                for t, new in enumerate(news):
                    s = piece * CHUNK + t
                    value[level * CAP + s] = new
                    leaving[step, s] = new
                    solved[step * SPAN + OWN * CAP + s] = new
                act = functools.partial(send, piece, p == PIECES // 2 - 1)
                if inverted:
                    pl.when(step < STEPS)(act)
                else:
                    act()
            return 0

        lax.fori_loop(0, 2, half, 0)
        if inverted:
            pl.when(step < STEPS)(lambda: send_sibling(step))
        else:
            send_sibling(step)

    def place_values(level, number, first):
        for t in range(CAP):
            here = right[table[ROW, number * CAP + t]]
            value[level * CAP + t] = here
            if first:
                leaving[0, t] = here
                solved[OWN * CAP + t] = here

    load_table.wait()
    load_right.wait()
    place_values(0, 5, True)
    pl.semaphore_wait(barrier, 1 + has_near.astype(jnp.int32) + has_far.astype(jnp.int32))
    for piece in range(PIECES):
        send_near(0, piece)
    send_far(0, 0, CAP)
    send_sibling(0)
    fill_terms(me, parity, count, level_ref, neighbor_ref, rows, place, table_v)
    load_table.start()
    load_table.wait()
    for level in (1, 2, 3):
        place_values(level, level - 1, False)
    load_off.wait()
    load_inverse.wait()

    def forward_step(step, _):
        receive(step - 1)
        solve(step, step, False)
        return 0

    def backward_step(step, _):
        receive(step - 1)
        solve(step, STEPS - step, True)
        return 0

    lax.fori_loop(1, 3, forward_step, 0)
    lax.fori_loop(3, STEPS + 1, backward_step, 0)

    for i in range(rows):
        out_ref[i] = value[table[PLACE, i]]

    def sent(kind):
        def one(step, _):
            there = section(step, SIBLING)
            remote(there, there, kind, step, sibling, near_sem.at[step, 0]).wait_send()
            return 0

        lax.fori_loop(0, STEPS, one, 0)

    sent(0)

    @pl.when(has_near)
    def _():
        sent(1)

    @pl.when(has_far)
    def _():
        sent(2)
        sent(3)


def local(count, right_sides, off_blocks, diag_inv, neighbors, level_of):
    width, blk = right_sides.shape[1:]

    def slots(*sizes):
        return pltpu.VMEM((*sizes, width, blk), jnp.bfloat16)

    return pl.pallas_call(
        functools.partial(kernel, count),
        out_shape=pltpu.VMEM(right_sides.shape, jnp.bfloat16),
        in_specs=[pl.BlockSpec(memory_space=pltpu.VMEM)] * 2 + [pl.BlockSpec(memory_space=pl.ANY)] * 3,
        out_specs=pl.BlockSpec(memory_space=pltpu.VMEM),
        scratch_shapes=[
            pltpu.VMEM(right_sides.shape, jnp.bfloat16),
            pltpu.VMEM(off_blocks.shape, jnp.bfloat16),
            pltpu.VMEM(diag_inv.shape, jnp.bfloat16),
            pltpu.VMEM((8, 128), jnp.int32),
            pltpu.SMEM((8, 128), jnp.int32),
            slots(LEVELS * CAP),
            slots((STEPS + 1) * SPAN),
            slots(STEPS + 1, CAP),
            slots(STEPS, 4 * CAP),
            pltpu.SemaphoreType.DMA((4,)),
            pltpu.SemaphoreType.DMA((4, STEPS)),
            pltpu.SemaphoreType.DMA((STEPS, PIECES)),
            pltpu.SemaphoreType.DMA((STEPS, 3)),
        ],
        compiler_params=pltpu.CompilerParams(
            collective_id=0, has_side_effects=True, vmem_limit_bytes=56 * 1024 * 1024
        ),
        cost_estimate=pl.CostEstimate(flops=600_000_000, bytes_accessed=7_000_000, transcendentals=0),
    )(level_of.reshape(-1, 128), neighbors.T, right_sides, off_blocks, diag_inv)


def solution(mesh):
    in_specs = (
        P("space", "rhs", None),
        P("space", None, None, None),
        P("space", None, None),
        P("space", None),
        P(),
    )
    return jax.shard_map(
        functools.partial(local, mesh.shape["space"]),
        mesh=mesh, in_specs=in_specs, out_specs=P("space", "rhs", None), check_vma=False,
    )
```

```python
import functools

import jax
import jax.numpy as jnp
from jax import lax
from jax.experimental import pallas as pl
from jax.experimental.pallas import tpu as pltpu
from jax.sharding import PartitionSpec as P

MESH = pl.DeviceIdType.MESH
LEVELS = 4
REACH = 2
NEIGH = 5
CAP = 16
STEPS = 6
CHUNK = 4
PIECES = CAP // CHUNK
SIBLING, NEAR, FAR, PASSED, OWN = range(5)
SPAN = 5 * CAP
ZERO = STEPS * SPAN
ROW, PLACE = NEIGH, NEIGH + 1


def window(me, count, level_ref, rows):
    per_line = 128 // rows
    across = lax.broadcasted_iota(jnp.int32, (rows, rows), 1)
    down = lax.broadcasted_iota(jnp.int32, (rows, rows), 0)

    def stand(row):
        return jnp.sum(jnp.where(across == down, row, 0), axis=1, keepdims=True)

    def levels(offset):
        device = jnp.clip(me + offset, 0, count - 1)
        line = level_ref[pl.ds(device // per_line, 1), :]
        part = device % per_line
        here = jnp.zeros((1, rows), jnp.int32)
        for t in range(per_line):
            here = jnp.where(part == t, line[:, t * rows : (t + 1) * rows], here)
        here = jnp.broadcast_to(here, (rows, rows))
        return here, stand(here)

    def ranks(here, column):
        earlier = jnp.where((column == here) & (down < across), 1, 0)
        return jnp.minimum(jnp.sum(earlier, axis=0, keepdims=True), CAP - 1)

    return across, down, stand, levels, ranks


def columns():
    lane = lax.broadcasted_iota(jnp.int32, (1, 128), 1)
    number = lane // CAP
    return lane, number, jnp.where(number < 3, number + 1, 5 - number)


def fill_rows(me, count, level_ref, rows, table_ref):
    across, down, _, levels, ranks = window(me, count, level_ref, rows)
    here, column = levels(0)
    earlier = jnp.where((column == here) & (across < down), 1, 0)
    slot = column * CAP + jnp.sum(earlier, axis=1, keepdims=True)
    lane, _, solves = columns()
    place = slot == jnp.broadcast_to(solves * CAP + lane % CAP, (rows, 128))
    number = lax.broadcasted_iota(jnp.int32, (rows, 128), 0)
    row_of = jnp.sum(jnp.where(place, number, 0), axis=0, keepdims=True)
    table_ref[ROW : ROW + 1, :] = jnp.clip(row_of, 0, rows - 1)
    table_ref[PLACE : PLACE + 1, 0:rows] = jnp.clip(here[0:1, :] * CAP + ranks(here, column), 0, LEVELS * CAP - 1)
    return place


def fill_terms(me, parity, count, level_ref, neighbor_ref, rows, place, table_ref):
    across, _, stand, levels, ranks = window(me, count, level_ref, rows)
    _, number, solves = columns()
    sections = {-2: FAR - parity, -1: PASSED - 3 * parity, 0: OWN, 1: 3 * parity, 2: NEAR + parity}
    codes = []
    for offset in range(-REACH, REACH + 1):
        here, column = levels(offset)
        codes.append(here * 128 + ranks(here, column) + sections[offset] * CAP)
    for k in range(NEIGH):
        row = jnp.broadcast_to(neighbor_ref[k : k + 1, :], (rows, rows))
        which = stand(row) - (me - REACH) * rows
        found = jnp.zeros((rows, rows), jnp.int32)
        for j in range(2 * REACH + 1):
            found += jnp.where(which - j * rows == across, codes[j], 0)
        code = jnp.sum(found, axis=1, keepdims=True)
        by_slot = jnp.sum(jnp.where(place, code, 0), axis=0, keepdims=True)
        spot, level = by_slot & 127, by_slot >> 7
        lower = (number < 3) & (level < solves)
        upper = (number >= 3) & (level > solves)
        index = jnp.where(lower, level * SPAN + spot, jnp.where(upper, (STEPS - level) * SPAN + spot, ZERO))
        table_ref[k : k + 1, :] = jnp.clip(index, 0, ZERO)


def kernel(count, level_hbm, neighbor_hbm, right_hbm, off_hbm, inverse_hbm, out_ref,
           level_ref, neighbor_ref, right, off, inverse, table_v, table, value, solved, leaving, arriving,
           load_sem, send_sem, near_sem, other_sem):
    load_level = pltpu.make_async_copy(level_hbm, level_ref, load_sem.at[4])
    load_level.start()
    me = lax.axis_index("space")
    parity = lax.rem(me, 2)
    sibling = me + 1 - 2 * parity
    to_near, to_far = me - 2 + 4 * parity, me + 2 - 4 * parity
    has_near = (to_near >= 0) & (to_near < count)
    has_far = (to_far >= 0) & (to_far < count)

    barrier = pltpu.get_barrier_semaphore()

    def greet(*targets):
        for target in targets:
            pl.semaphore_signal(barrier, inc=1, device_id={"space": target}, device_id_type=MESH)

    greet(sibling)
    pl.when(has_near)(lambda: greet(to_near))
    pl.when(has_far)(lambda: greet(to_far))

    rows = right.shape[0]
    load_right = pltpu.make_async_copy(right_hbm, right, load_sem.at[0])
    load_right.start()
    load_neighbor = pltpu.make_async_copy(neighbor_hbm, neighbor_ref, load_sem.at[5])
    load_neighbor.start()
    for start in range(0, rows, 4):
        part = pl.ds(start, 4)
        pltpu.make_async_copy(off_hbm.at[part], off.at[part], load_sem.at[1]).start()
    load_off = pltpu.make_async_copy(off_hbm, off, load_sem.at[1])
    load_inverse = pltpu.make_async_copy(inverse_hbm, inverse, load_sem.at[2])
    load_inverse.start()
    load_table = pltpu.make_async_copy(table_v, table, load_sem.at[3])

    table_v[...] = jnp.zeros_like(table_v)
    load_level.wait()
    place = fill_rows(me, count, level_ref, rows, table_v)
    load_table.start()
    solved[ZERO] = jnp.zeros(solved.shape[1:], solved.dtype)

    def remote(source, target, kind, step, to, sem):
        return pltpu.make_async_remote_copy(
            src_ref=source, dst_ref=target, send_sem=send_sem.at[kind, step], recv_sem=sem,
            device_id={"space": to}, device_id_type=MESH,
        )

    def section(step, which, start=0, size=CAP):
        return arriving.at[step, pl.ds(which * CAP + start, size)]

    def own(step, start=0, size=CAP):
        return leaving.at[step, pl.ds(start, size)]

    def send_near(step, piece):
        at = piece * CHUNK

        @pl.when(has_near)
        def _():
            remote(own(step, at, CHUNK), section(step, NEAR, at, CHUNK), 1, step, to_near,
                   near_sem.at[step, piece]).start()

    def send_rest(step):
        @pl.when(has_far)
        def _():
            remote(own(step), section(step, FAR), 2, step, to_far, other_sem.at[step, 1]).start()

        remote(own(step), section(step, SIBLING), 0, step, sibling, other_sem.at[step, 0]).start()

    def sent(step):
        def wait(kind):
            there = section(step, SIBLING)
            remote(there, there, kind, step, sibling, near_sem.at[step, 0]).wait_send()

        wait(0)

        @pl.when(has_near)
        def _():
            wait(1)

        @pl.when(has_far)
        def _():
            wait(2)
            wait(3)

    def arrived(step, which, start, size, sem):
        there = section(step, which, start, size)
        remote(there, there, 0, step, sibling, sem).wait_recv()

    def keep(step, which):
        solved[pl.ds(step * SPAN + which * CAP, CAP)] = arriving[step, pl.ds(which * CAP, CAP)]

    def receive(step):
        @pl.when(has_far)
        def _():
            for piece in range(PIECES):
                at = piece * CHUNK
                arrived(step, NEAR, at, CHUNK, near_sem.at[step, piece])
                remote(section(step, NEAR, at, CHUNK), section(step, PASSED, at, CHUNK), 3, step, sibling,
                       other_sem.at[step, 2]).start()
            keep(step, NEAR)

        arrived(step, SIBLING, 0, CAP, other_sem.at[step, 0])
        keep(step, SIBLING)

        @pl.when(has_near)
        def _():
            arrived(step, FAR, 0, CAP, other_sem.at[step, 1])
            keep(step, FAR)
            arrived(step, PASSED, 0, CAP, other_sem.at[step, 2])
            keep(step, PASSED)

    def paired(lefts, blocks):
        both = lax.dot_general(
            jnp.concatenate(lefts, axis=0), jnp.concatenate(blocks, axis=0),
            (((1,), (1,)), ((), ())), preferred_element_type=jnp.float32,
        )
        height, width = lefts[0].shape[0], blocks[0].shape[0]
        return both[:height, :width], both[height:, width:]

    def solve(step, level, inverted):
        def pair(s):
            ats = [(step - 1) * CAP + s + t for t in range(2)]
            two = [table[ROW, at] for at in ats]
            lefts = [jnp.concatenate([solved[table[k, at]] for k in range(NEIGH)], axis=1) for at in ats]
            blocks = [jnp.concatenate([off[row, k] for k in range(NEIGH)], axis=1) for row in two]
            news = [
                (value[level * CAP + s + t].astype(jnp.float32) - total).astype(jnp.bfloat16)
                for t, total in enumerate(paired(lefts, blocks))
            ]
            if inverted:
                news = [new.astype(jnp.bfloat16) for new in paired(news, [inverse[row] for row in two])]
            return news

        def half(h, _):
            for p in range(PIECES // 2):
                piece = h * (PIECES // 2) + p
                news = sum([pair(piece * CHUNK + t) for t in range(0, CHUNK, 2)], [])
                for t, new in enumerate(news):
                    s = piece * CHUNK + t
                    value[level * CAP + s] = new
                    leaving[step, s] = new
                    solved[step * SPAN + OWN * CAP + s] = new
                if inverted:
                    pl.when(step < STEPS)(functools.partial(send_near, step, piece))
                else:
                    send_near(step, piece)
            return 0

        lax.fori_loop(0, 2, half, 0)
        if inverted:
            pl.when(step < STEPS)(functools.partial(send_rest, step))
        else:
            send_rest(step)
        sent(step - 1)

    def place_values(level, number, first):
        for t in range(CAP):
            here = right[table[ROW, number * CAP + t]]
            value[level * CAP + t] = here
            if first:
                leaving[0, t] = here
                solved[OWN * CAP + t] = here

    load_table.wait()
    load_right.wait()
    place_values(0, 5, True)
    pl.semaphore_wait(barrier, 1 + has_near.astype(jnp.int32) + has_far.astype(jnp.int32))
    for piece in range(PIECES):
        send_near(0, piece)
    send_rest(0)
    load_neighbor.wait()
    fill_terms(me, parity, count, level_ref, neighbor_ref, rows, place, table_v)
    load_table.start()
    load_table.wait()
    for level in (1, 2, 3):
        place_values(level, level - 1, False)
    load_off.wait()
    load_inverse.wait()

    def forward_step(step, _):
        receive(step - 1)
        solve(step, step, False)
        return 0

    def backward_step(step, _):
        receive(step - 1)
        solve(step, STEPS - step, True)
        return 0

    lax.fori_loop(1, 3, forward_step, 0)
    lax.fori_loop(3, STEPS + 1, backward_step, 0)

    for i in range(rows):
        out_ref[i] = value[table[PLACE, i]]


def local(count, right_sides, off_blocks, diag_inv, neighbors, level_of):
    width, blk = right_sides.shape[1:]

    def slots(*sizes):
        return pltpu.VMEM((*sizes, width, blk), jnp.bfloat16)

    return pl.pallas_call(
        functools.partial(kernel, count),
        out_shape=pltpu.VMEM(right_sides.shape, jnp.bfloat16),
        in_specs=[pl.BlockSpec(memory_space=pl.ANY)] * 5,
        out_specs=pl.BlockSpec(memory_space=pltpu.VMEM),
        scratch_shapes=[
            pltpu.VMEM((level_of.shape[0] // 128, 128), jnp.int32),
            pltpu.VMEM(neighbors.shape[::-1], jnp.int32),
            pltpu.VMEM(right_sides.shape, jnp.bfloat16),
            pltpu.VMEM(off_blocks.shape, jnp.bfloat16),
            pltpu.VMEM(diag_inv.shape, jnp.bfloat16),
            pltpu.VMEM((8, 128), jnp.int32),
            pltpu.SMEM((8, 128), jnp.int32),
            slots(LEVELS * CAP),
            slots((STEPS + 1) * SPAN),
            slots(STEPS + 1, CAP),
            slots(STEPS, 4 * CAP),
            pltpu.SemaphoreType.DMA((6,)),
            pltpu.SemaphoreType.DMA((4, STEPS)),
            pltpu.SemaphoreType.DMA((STEPS, PIECES)),
            pltpu.SemaphoreType.DMA((STEPS, 3)),
        ],
        compiler_params=pltpu.CompilerParams(
            collective_id=0, has_side_effects=True, vmem_limit_bytes=56 * 1024 * 1024
        ),
        cost_estimate=pl.CostEstimate(flops=600_000_000, bytes_accessed=7_000_000, transcendentals=0),
    )(level_of.reshape(-1, 128), neighbors.T, right_sides, off_blocks, diag_inv)


def solution(mesh):
    in_specs = (
        P("space", "rhs", None),
        P("space", None, None, None),
        P("space", None, None),
        P("space", None),
        P(),
    )
    return jax.shard_map(
        functools.partial(local, mesh.shape["space"]),
        mesh=mesh, in_specs=in_specs, out_specs=P("space", "rhs", None), check_vma=False,
    )
```

```python
import functools

import jax
import jax.numpy as jnp
from jax import lax
from jax.experimental import pallas as pl
from jax.experimental.pallas import tpu as pltpu
from jax.sharding import PartitionSpec as P

MESH = pl.DeviceIdType.MESH
LEVELS = 4
REACH = 2
NEIGH = 5
CAP = 16
STEPS = 6
CHUNK = 4
PIECES = CAP // CHUNK
PASSED_ON = 3
SIBLING, NEAR, FAR, PASSED, OWN = range(5)
SPAN = 5 * CAP
ZERO = STEPS * SPAN
ROW, PLACE = NEIGH, NEIGH + 1


def window(me, count, level_ref, rows):
    per_line = 128 // rows
    across = lax.broadcasted_iota(jnp.int32, (rows, rows), 1)
    down = lax.broadcasted_iota(jnp.int32, (rows, rows), 0)

    def stand(row):
        return jnp.sum(jnp.where(across == down, row, 0), axis=1, keepdims=True)

    def levels(offset):
        device = jnp.clip(me + offset, 0, count - 1)
        line = level_ref[pl.ds(device // per_line, 1), :]
        part = device % per_line
        here = jnp.zeros((1, rows), jnp.int32)
        for t in range(per_line):
            here = jnp.where(part == t, line[:, t * rows : (t + 1) * rows], here)
        here = jnp.broadcast_to(here, (rows, rows))
        return here, stand(here)

    def ranks(here, column):
        earlier = jnp.where((column == here) & (down < across), 1, 0)
        return jnp.minimum(jnp.sum(earlier, axis=0, keepdims=True), CAP - 1)

    return across, down, stand, levels, ranks


def columns():
    lane = lax.broadcasted_iota(jnp.int32, (1, 128), 1)
    number = lane // CAP
    return lane, number, jnp.where(number < 3, number + 1, 5 - number)


def fill_rows(me, count, level_ref, rows, table_ref):
    across, down, _, levels, ranks = window(me, count, level_ref, rows)
    here, column = levels(0)
    earlier = jnp.where((column == here) & (across < down), 1, 0)
    slot = column * CAP + jnp.sum(earlier, axis=1, keepdims=True)
    lane, _, solves = columns()
    place = slot == jnp.broadcast_to(solves * CAP + lane % CAP, (rows, 128))
    number = lax.broadcasted_iota(jnp.int32, (rows, 128), 0)
    row_of = jnp.sum(jnp.where(place, number, 0), axis=0, keepdims=True)
    table_ref[ROW : ROW + 1, :] = jnp.clip(row_of, 0, rows - 1)
    table_ref[PLACE : PLACE + 1, 0:rows] = jnp.clip(here[0:1, :] * CAP + ranks(here, column), 0, LEVELS * CAP - 1)
    return place


def fill_terms(me, parity, count, level_ref, neighbor_ref, rows, place, table_ref):
    across, _, stand, levels, ranks = window(me, count, level_ref, rows)
    _, number, solves = columns()
    sections = {-2: FAR - parity, -1: PASSED - 3 * parity, 0: OWN, 1: 3 * parity, 2: NEAR + parity}
    codes = []
    for offset in range(-REACH, REACH + 1):
        here, column = levels(offset)
        codes.append(here * 128 + ranks(here, column) + sections[offset] * CAP)
    for k in range(NEIGH):
        row = jnp.broadcast_to(neighbor_ref[k : k + 1, :], (rows, rows))
        which = stand(row) - (me - REACH) * rows
        found = jnp.zeros((rows, rows), jnp.int32)
        for j in range(2 * REACH + 1):
            found += jnp.where(which - j * rows == across, codes[j], 0)
        code = jnp.sum(found, axis=1, keepdims=True)
        by_slot = jnp.sum(jnp.where(place, code, 0), axis=0, keepdims=True)
        spot, level = by_slot & 127, by_slot >> 7
        lower = (number < 3) & (level < solves)
        upper = (number >= 3) & (level > solves)
        index = jnp.where(lower, level * SPAN + spot, jnp.where(upper, (STEPS - level) * SPAN + spot, ZERO))
        table_ref[k : k + 1, :] = jnp.clip(index, 0, ZERO)


def kernel(count, level_hbm, neighbor_hbm, right_hbm, off_hbm, inverse_hbm, out_ref,
           level_ref, neighbor_ref, right, off, inverse, table_v, table, value, solved, leaving, arriving,
           load_sem, send_sem, near_sem, other_sem):
    load_level = pltpu.make_async_copy(level_hbm, level_ref, load_sem.at[4])
    load_level.start()
    me = lax.axis_index("space")
    parity = lax.rem(me, 2)
    sibling = me + 1 - 2 * parity
    to_near, to_cross, to_far = me - 2 + 4 * parity, me - 1 + 2 * parity, me + 2 - 4 * parity
    has_near = (to_near >= 0) & (to_near < count)
    has_far = (to_far >= 0) & (to_far < count)

    barrier = pltpu.get_barrier_semaphore()

    def greet(*targets):
        for target in targets:
            pl.semaphore_signal(barrier, inc=1, device_id={"space": target}, device_id_type=MESH)

    greet(sibling)
    pl.when(has_near)(lambda: greet(to_near, to_cross))
    pl.when(has_far)(lambda: greet(to_far))

    rows = right.shape[0]
    load_right = pltpu.make_async_copy(right_hbm, right, load_sem.at[0])
    load_right.start()
    load_neighbor = pltpu.make_async_copy(neighbor_hbm, neighbor_ref, load_sem.at[5])
    load_neighbor.start()
    for start in range(0, rows, 4):
        part = pl.ds(start, 4)
        pltpu.make_async_copy(off_hbm.at[part], off.at[part], load_sem.at[1]).start()
    load_off = pltpu.make_async_copy(off_hbm, off, load_sem.at[1])
    load_inverse = pltpu.make_async_copy(inverse_hbm, inverse, load_sem.at[2])
    load_inverse.start()
    load_table = pltpu.make_async_copy(table_v, table, load_sem.at[3])

    table_v[...] = jnp.zeros_like(table_v)
    load_level.wait()
    place = fill_rows(me, count, level_ref, rows, table_v)
    load_table.start()
    solved[ZERO] = jnp.zeros(solved.shape[1:], solved.dtype)

    def remote(source, target, kind, step, to, sem):
        return pltpu.make_async_remote_copy(
            src_ref=source, dst_ref=target, send_sem=send_sem.at[kind, step], recv_sem=sem,
            device_id={"space": to}, device_id_type=MESH,
        )

    def section(step, which, start=0, size=CAP):
        return arriving.at[step, pl.ds(which * CAP + start, size)]

    def own(step, start=0, size=CAP):
        return leaving.at[step, pl.ds(start, size)]

    def send_near(step, piece):
        at = piece * CHUNK

        @pl.when(has_near)
        def _():
            remote(own(step, at, CHUNK), section(step, NEAR, at, CHUNK), 1, step, to_near,
                   near_sem.at[step, piece]).start()

            @pl.when(piece >= PASSED_ON)
            def _():
                remote(own(step, at, CHUNK), section(step, PASSED, at, CHUNK), 4, step, to_cross,
                       other_sem.at[step, 3]).start()

    def send_rest(step):
        @pl.when(has_far)
        def _():
            remote(own(step), section(step, FAR), 2, step, to_far, other_sem.at[step, 1]).start()

        remote(own(step), section(step, SIBLING), 0, step, sibling, other_sem.at[step, 0]).start()

    def sent(step):
        def wait(kind, pieces=PIECES):
            there = section(step, SIBLING, 0, pieces * CHUNK)
            remote(there, there, kind, step, sibling, near_sem.at[step, 0]).wait_send()

        wait(0)

        @pl.when(has_near)
        def _():
            wait(1)
            wait(4, PIECES - PASSED_ON)

        @pl.when(has_far)
        def _():
            wait(2)
            wait(3, PASSED_ON)

    def arrived(step, which, start, size, sem):
        there = section(step, which, start, size)
        remote(there, there, 0, step, sibling, sem).wait_recv()

    def keep(step, which):
        solved[pl.ds(step * SPAN + which * CAP, CAP)] = arriving[step, pl.ds(which * CAP, CAP)]

    def receive(step):
        @pl.when(has_far)
        def _():
            for piece in range(PIECES):
                at = piece * CHUNK
                arrived(step, NEAR, at, CHUNK, near_sem.at[step, piece])
                if piece < PASSED_ON:
                    remote(section(step, NEAR, at, CHUNK), section(step, PASSED, at, CHUNK), 3, step, sibling,
                           other_sem.at[step, 2]).start()
            keep(step, NEAR)

        arrived(step, SIBLING, 0, CAP, other_sem.at[step, 0])
        keep(step, SIBLING)

        @pl.when(has_near)
        def _():
            arrived(step, FAR, 0, CAP, other_sem.at[step, 1])
            keep(step, FAR)
            arrived(step, PASSED, 0, PASSED_ON * CHUNK, other_sem.at[step, 2])
            arrived(step, PASSED, PASSED_ON * CHUNK, CAP - PASSED_ON * CHUNK, other_sem.at[step, 3])
            keep(step, PASSED)

    def paired(lefts, blocks):
        both = lax.dot_general(
            jnp.concatenate(lefts, axis=0), jnp.concatenate(blocks, axis=0),
            (((1,), (1,)), ((), ())), preferred_element_type=jnp.float32,
        )
        height, width = lefts[0].shape[0], blocks[0].shape[0]
        return both[:height, :width], both[height:, width:]

    def solve(step, level, inverted):
        def pair(s):
            ats = [(step - 1) * CAP + s + t for t in range(2)]
            two = [table[ROW, at] for at in ats]
            lefts = [jnp.concatenate([solved[table[k, at]] for k in range(NEIGH)], axis=1) for at in ats]
            blocks = [jnp.concatenate([off[row, k] for k in range(NEIGH)], axis=1) for row in two]
            news = [
                (value[level * CAP + s + t].astype(jnp.float32) - total).astype(jnp.bfloat16)
                for t, total in enumerate(paired(lefts, blocks))
            ]
            if inverted:
                news = [new.astype(jnp.bfloat16) for new in paired(news, [inverse[row] for row in two])]
            return news

        def half(h, _):
            for p in range(PIECES // 2):
                piece = h * (PIECES // 2) + p
                news = sum([pair(piece * CHUNK + t) for t in range(0, CHUNK, 2)], [])
                for t, new in enumerate(news):
                    s = piece * CHUNK + t
                    value[level * CAP + s] = new
                    leaving[step, s] = new
                    solved[step * SPAN + OWN * CAP + s] = new
                if inverted:
                    pl.when(step < STEPS)(functools.partial(send_near, step, piece))
                else:
                    send_near(step, piece)
            return 0

        lax.fori_loop(0, 2, half, 0)
        if inverted:
            pl.when(step < STEPS)(functools.partial(send_rest, step))
        else:
            send_rest(step)
        sent(step - 1)

    def place_values(level, number, first):
        for t in range(CAP):
            here = right[table[ROW, number * CAP + t]]
            value[level * CAP + t] = here
            if first:
                leaving[0, t] = here
                solved[OWN * CAP + t] = here

    load_table.wait()
    load_right.wait()
    place_values(0, 5, True)
    pl.semaphore_wait(barrier, 1 + 2 * has_near.astype(jnp.int32) + has_far.astype(jnp.int32))
    for piece in range(PIECES):
        send_near(0, piece)
    send_rest(0)
    load_neighbor.wait()
    fill_terms(me, parity, count, level_ref, neighbor_ref, rows, place, table_v)
    load_table.start()
    load_table.wait()
    for level in (1, 2, 3):
        place_values(level, level - 1, False)
    load_off.wait()
    load_inverse.wait()

    def forward_step(step, _):
        receive(step - 1)
        solve(step, step, False)
        return 0

    def backward_step(step, _):
        receive(step - 1)
        solve(step, STEPS - step, True)
        return 0

    lax.fori_loop(1, 3, forward_step, 0)
    lax.fori_loop(3, STEPS + 1, backward_step, 0)

    for i in range(rows):
        out_ref[i] = value[table[PLACE, i]]


def local(count, right_sides, off_blocks, diag_inv, neighbors, level_of):
    width, blk = right_sides.shape[1:]

    def slots(*sizes):
        return pltpu.VMEM((*sizes, width, blk), jnp.bfloat16)

    return pl.pallas_call(
        functools.partial(kernel, count),
        out_shape=pltpu.VMEM(right_sides.shape, jnp.bfloat16),
        in_specs=[pl.BlockSpec(memory_space=pl.ANY)] * 5,
        out_specs=pl.BlockSpec(memory_space=pltpu.VMEM),
        scratch_shapes=[
            pltpu.VMEM((level_of.shape[0] // 128, 128), jnp.int32),
            pltpu.VMEM(neighbors.shape[::-1], jnp.int32),
            pltpu.VMEM(right_sides.shape, jnp.bfloat16),
            pltpu.VMEM(off_blocks.shape, jnp.bfloat16),
            pltpu.VMEM(diag_inv.shape, jnp.bfloat16),
            pltpu.VMEM((8, 128), jnp.int32),
            pltpu.SMEM((8, 128), jnp.int32),
            slots(LEVELS * CAP),
            slots((STEPS + 1) * SPAN),
            slots(STEPS + 1, CAP),
            slots(STEPS, 4 * CAP),
            pltpu.SemaphoreType.DMA((6,)),
            pltpu.SemaphoreType.DMA((5, STEPS)),
            pltpu.SemaphoreType.DMA((STEPS, PIECES)),
            pltpu.SemaphoreType.DMA((STEPS, 4)),
        ],
        compiler_params=pltpu.CompilerParams(
            collective_id=0, has_side_effects=True, vmem_limit_bytes=56 * 1024 * 1024
        ),
        cost_estimate=pl.CostEstimate(flops=600_000_000, bytes_accessed=7_000_000, transcendentals=0),
    )(level_of.reshape(-1, 128), neighbors.T, right_sides, off_blocks, diag_inv)


def solution(mesh):
    in_specs = (
        P("space", "rhs", None),
        P("space", None, None, None),
        P("space", None, None),
        P("space", None),
        P(),
    )
    return jax.shard_map(
        functools.partial(local, mesh.shape["space"]),
        mesh=mesh, in_specs=in_specs, out_specs=P("space", "rhs", None), check_vma=False,
    )
```

```python
import functools

import jax
import jax.numpy as jnp
from jax import lax
from jax.experimental import pallas as pl
from jax.experimental.pallas import tpu as pltpu
from jax.sharding import PartitionSpec as P

MESH = pl.DeviceIdType.MESH
LEVELS = 4
REACH = 2
NEIGH = 5
CAP = 16
STEPS = 6
CHUNK = 4
PIECES = CAP // CHUNK
SIBLING, NEAR, FAR, PASSED, OWN = range(5)
SPARE = 4
SPAN = 5 * CAP
ZERO = STEPS * SPAN
ROW, PLACE = NEIGH, NEIGH + 1


def window(me, count, level_ref, rows):
    per_line = 128 // rows
    across = lax.broadcasted_iota(jnp.int32, (rows, rows), 1)
    down = lax.broadcasted_iota(jnp.int32, (rows, rows), 0)

    def stand(row):
        return jnp.sum(jnp.where(across == down, row, 0), axis=1, keepdims=True)

    def levels(offset):
        device = jnp.clip(me + offset, 0, count - 1)
        line = level_ref[pl.ds(device // per_line, 1), :]
        part = device % per_line
        here = jnp.zeros((1, rows), jnp.int32)
        for t in range(per_line):
            here = jnp.where(part == t, line[:, t * rows : (t + 1) * rows], here)
        here = jnp.broadcast_to(here, (rows, rows))
        return here, stand(here)

    def ranks(here, column):
        earlier = jnp.where((column == here) & (down < across), 1, 0)
        return jnp.minimum(jnp.sum(earlier, axis=0, keepdims=True), CAP - 1)

    return across, down, stand, levels, ranks


def columns():
    lane = lax.broadcasted_iota(jnp.int32, (1, 128), 1)
    number = lane // CAP
    return lane, number, jnp.where(number < 3, number + 1, 5 - number)


def fill_rows(me, count, level_ref, rows, table_ref):
    across, down, _, levels, ranks = window(me, count, level_ref, rows)
    here, column = levels(0)
    earlier = jnp.where((column == here) & (across < down), 1, 0)
    slot = column * CAP + jnp.sum(earlier, axis=1, keepdims=True)
    lane, _, solves = columns()
    place = slot == jnp.broadcast_to(solves * CAP + lane % CAP, (rows, 128))
    number = lax.broadcasted_iota(jnp.int32, (rows, 128), 0)
    row_of = jnp.sum(jnp.where(place, number, 0), axis=0, keepdims=True)
    table_ref[ROW : ROW + 1, :] = jnp.clip(row_of, 0, rows - 1)
    table_ref[PLACE : PLACE + 1, 0:rows] = jnp.clip(here[0:1, :] * CAP + ranks(here, column), 0, LEVELS * CAP - 1)
    return place


def fill_terms(me, parity, count, level_ref, neighbor_ref, rows, place, table_ref):
    across, _, stand, levels, ranks = window(me, count, level_ref, rows)
    _, number, solves = columns()
    sections = {-2: FAR - parity, -1: PASSED - 3 * parity, 0: OWN, 1: 3 * parity, 2: NEAR + parity}
    codes = []
    for offset in range(-REACH, REACH + 1):
        here, column = levels(offset)
        codes.append(here * 128 + ranks(here, column) + sections[offset] * CAP)
    for k in range(NEIGH):
        row = jnp.broadcast_to(neighbor_ref[k : k + 1, :], (rows, rows))
        which = stand(row) - (me - REACH) * rows
        found = jnp.zeros((rows, rows), jnp.int32)
        for j in range(2 * REACH + 1):
            found += jnp.where(which - j * rows == across, codes[j], 0)
        code = jnp.sum(found, axis=1, keepdims=True)
        by_slot = jnp.sum(jnp.where(place, code, 0), axis=0, keepdims=True)
        spot, level = by_slot & 127, by_slot >> 7
        lower = (number < 3) & (level < solves)
        upper = (number >= 3) & (level > solves)
        index = jnp.where(lower, level * SPAN + spot, jnp.where(upper, (STEPS - level) * SPAN + spot, ZERO))
        table_ref[k : k + 1, :] = jnp.clip(index, 0, ZERO)


def kernel(count, level_hbm, neighbor_hbm, right_hbm, off_hbm, inverse_hbm, out_ref,
           level_ref, neighbor_ref, right, off, inverse, table_v, table, value, solved, leaving, arriving,
           load_sem, send_sem, near_sem, other_sem):
    load_level = pltpu.make_async_copy(level_hbm, level_ref, load_sem.at[4])
    load_level.start()
    me = lax.axis_index("space")
    parity = lax.rem(me, 2)
    sibling = me + 1 - 2 * parity
    to_near, to_far = me - 2 + 4 * parity, me + 2 - 4 * parity
    has_near = (to_near >= 0) & (to_near < count)
    has_far = (to_far >= 0) & (to_far < count)

    near_there, far_there = has_near.astype(jnp.int32), has_far.astype(jnp.int32)
    near_to = sibling + near_there * (to_near - sibling)
    near_at = (SPARE + near_there * (NEAR - SPARE)) * CAP
    far_to = sibling + far_there * (to_far - sibling)
    far_at = (SPARE + far_there * (FAR - SPARE)) * CAP

    barrier = pltpu.get_barrier_semaphore()

    def greet(*targets):
        for target in targets:
            pl.semaphore_signal(barrier, inc=1, device_id={"space": target}, device_id_type=MESH)

    greet(sibling)
    pl.when(has_near)(lambda: greet(to_near))
    pl.when(has_far)(lambda: greet(to_far))

    rows = right.shape[0]
    load_right = pltpu.make_async_copy(right_hbm, right, load_sem.at[0])
    load_right.start()
    load_neighbor = pltpu.make_async_copy(neighbor_hbm, neighbor_ref, load_sem.at[5])
    load_neighbor.start()
    for start in range(0, rows, 4):
        part = pl.ds(start, 4)
        pltpu.make_async_copy(off_hbm.at[part], off.at[part], load_sem.at[1]).start()
    load_off = pltpu.make_async_copy(off_hbm, off, load_sem.at[1])
    load_inverse = pltpu.make_async_copy(inverse_hbm, inverse, load_sem.at[2])
    load_inverse.start()
    load_table = pltpu.make_async_copy(table_v, table, load_sem.at[3])

    table_v[...] = jnp.zeros_like(table_v)
    load_level.wait()
    place = fill_rows(me, count, level_ref, rows, table_v)
    load_table.start()
    solved[ZERO] = jnp.zeros(solved.shape[1:], solved.dtype)

    def remote(source, target, kind, step, to, sem):
        return pltpu.make_async_remote_copy(
            src_ref=source, dst_ref=target, send_sem=send_sem.at[kind, step], recv_sem=sem,
            device_id={"space": to}, device_id_type=MESH,
        )

    def section(step, which, start=0, size=CAP):
        return arriving.at[step, pl.ds(which * CAP + start, size)]

    def own(step, start=0, size=CAP):
        return leaving.at[step, pl.ds(start, size)]

    def send_near(step, piece):
        at = piece * CHUNK
        remote(own(step, at, CHUNK), arriving.at[step, pl.ds(near_at + at, CHUNK)], 1, step, near_to,
               near_sem.at[step, near_there * piece + (1 - near_there) * PIECES]).start()

    def send_far(step, start, size):
        remote(own(step, start, size), arriving.at[step, pl.ds(far_at + start, size)], 2, step, far_to,
               other_sem.at[step, 3 - 2 * far_there]).start()

    def send_sibling(step):
        remote(own(step), section(step, SIBLING), 0, step, sibling, other_sem.at[step, 0]).start()

    def sent(step):
        def wait(kind):
            there = section(step, SIBLING)
            remote(there, there, kind, step, sibling, near_sem.at[step, 0]).wait_send()

        wait(0)
        wait(1)
        wait(2)
        pl.when(has_far)(lambda: wait(3))

    def arrived(step, which, start, size, sem):
        there = section(step, which, start, size)
        remote(there, there, 0, step, sibling, sem).wait_recv()

    def keep(step, which):
        solved[pl.ds(step * SPAN + which * CAP, CAP)] = arriving[step, pl.ds(which * CAP, CAP)]

    def receive(step):
        @pl.when(has_far)
        def _():
            for piece in range(PIECES):
                at = piece * CHUNK
                arrived(step, NEAR, at, CHUNK, near_sem.at[step, piece])
                remote(section(step, NEAR, at, CHUNK), section(step, PASSED, at, CHUNK), 3, step, sibling,
                       other_sem.at[step, 2]).start()
            keep(step, NEAR)

        @pl.when(jnp.logical_not(has_far))
        def _():
            arrived(step, SPARE, 0, CAP, near_sem.at[step, PIECES])

        @pl.when(jnp.logical_not(has_near))
        def _():
            arrived(step, SPARE, 0, CAP, other_sem.at[step, 3])

        arrived(step, SIBLING, 0, CAP, other_sem.at[step, 0])
        keep(step, SIBLING)

        @pl.when(has_near)
        def _():
            arrived(step, FAR, 0, CAP, other_sem.at[step, 1])
            keep(step, FAR)
            arrived(step, PASSED, 0, CAP, other_sem.at[step, 2])
            keep(step, PASSED)

    def paired(lefts, blocks):
        both = lax.dot_general(
            jnp.concatenate(lefts, axis=0), jnp.concatenate(blocks, axis=0),
            (((1,), (1,)), ((), ())), preferred_element_type=jnp.float32,
        )
        height, width = lefts[0].shape[0], blocks[0].shape[0]
        return both[:height, :width], both[height:, width:]

    def solve(step, level, inverted, leaves):
        def pair(s):
            ats = [(step - 1) * CAP + s + t for t in range(2)]
            two = [table[ROW, at] for at in ats]
            lefts = [jnp.concatenate([solved[table[k, at]] for k in range(NEIGH)], axis=1) for at in ats]
            blocks = [jnp.concatenate([off[row, k] for k in range(NEIGH)], axis=1) for row in two]
            news = [
                (value[level * CAP + s + t].astype(jnp.float32) - total).astype(jnp.bfloat16)
                for t, total in enumerate(paired(lefts, blocks))
            ]
            if inverted:
                news = [new.astype(jnp.bfloat16) for new in paired(news, [inverse[row] for row in two])]
            return news

        everything = []
        for piece in range(PIECES):
            news = sum([pair(piece * CHUNK + t) for t in range(0, CHUNK, 2)], [])
            for t, new in enumerate(news):
                value[level * CAP + piece * CHUNK + t] = new
                if leaves:
                    leaving[step, piece * CHUNK + t] = new
            everything += news
            if leaves:
                send_near(step, piece)
                if piece % 2 == 1:
                    send_far(step, (piece - 1) * CHUNK, 2 * CHUNK)
        if leaves:
            send_sibling(step)
            for t, new in enumerate(everything):
                solved[step * SPAN + OWN * CAP + t] = new
        sent(step - 1)

    def place_values(level, number, first):
        for t in range(CAP):
            here = right[table[ROW, number * CAP + t]]
            value[level * CAP + t] = here
            if first:
                leaving[0, t] = here
                solved[OWN * CAP + t] = here

    load_table.wait()
    load_right.wait()
    place_values(0, 5, True)
    pl.semaphore_wait(barrier, 1 + has_near.astype(jnp.int32) + has_far.astype(jnp.int32))
    for piece in range(PIECES):
        send_near(0, piece)
    send_far(0, 0, CAP)
    send_sibling(0)
    load_neighbor.wait()
    fill_terms(me, parity, count, level_ref, neighbor_ref, rows, place, table_v)
    load_table.start()
    load_table.wait()
    for level in (1, 2, 3):
        place_values(level, level - 1, False)
    load_off.wait()
    load_inverse.wait()

    def forward_step(step, _):
        receive(step - 1)
        solve(step, step, False, True)
        return 0

    def backward_step(step, _):
        receive(step - 1)
        solve(step, STEPS - step, True, True)
        return 0

    lax.fori_loop(1, 3, forward_step, 0)
    lax.fori_loop(3, STEPS, backward_step, 0)
    receive(STEPS - 1)
    solve(STEPS, 0, True, False)

    for i in range(rows):
        out_ref[i] = value[table[PLACE, i]]


def local(count, right_sides, off_blocks, diag_inv, neighbors, level_of):
    width, blk = right_sides.shape[1:]

    def slots(*sizes):
        return pltpu.VMEM((*sizes, width, blk), jnp.bfloat16)

    return pl.pallas_call(
        functools.partial(kernel, count),
        out_shape=pltpu.VMEM(right_sides.shape, jnp.bfloat16),
        in_specs=[pl.BlockSpec(memory_space=pl.ANY)] * 5,
        out_specs=pl.BlockSpec(memory_space=pltpu.VMEM),
        scratch_shapes=[
            pltpu.VMEM((level_of.shape[0] // 128, 128), jnp.int32),
            pltpu.VMEM(neighbors.shape[::-1], jnp.int32),
            pltpu.VMEM(right_sides.shape, jnp.bfloat16),
            pltpu.VMEM(off_blocks.shape, jnp.bfloat16),
            pltpu.VMEM(diag_inv.shape, jnp.bfloat16),
            pltpu.VMEM((8, 128), jnp.int32),
            pltpu.SMEM((8, 128), jnp.int32),
            slots(LEVELS * CAP),
            slots(STEPS * SPAN + 1),
            slots(STEPS, CAP),
            slots(STEPS, 5 * CAP),
            pltpu.SemaphoreType.DMA((6,)),
            pltpu.SemaphoreType.DMA((4, STEPS)),
            pltpu.SemaphoreType.DMA((STEPS, PIECES + 1)),
            pltpu.SemaphoreType.DMA((STEPS, 4)),
        ],
        compiler_params=pltpu.CompilerParams(
            collective_id=0, has_side_effects=True, vmem_limit_bytes=56 * 1024 * 1024
        ),
        cost_estimate=pl.CostEstimate(flops=600_000_000, bytes_accessed=7_000_000, transcendentals=0),
    )(level_of.reshape(-1, 128), neighbors.T, right_sides, off_blocks, diag_inv)


def solution(mesh):
    in_specs = (
        P("space", "rhs", None),
        P("space", None, None, None),
        P("space", None, None),
        P("space", None),
        P(),
    )
    return jax.shard_map(
        functools.partial(local, mesh.shape["space"]),
        mesh=mesh, in_specs=in_specs, out_specs=P("space", "rhs", None), check_vma=False,
    )
```

```python
import functools

import jax
import jax.numpy as jnp
from jax import lax
from jax.experimental import pallas as pl
from jax.experimental.pallas import tpu as pltpu
from jax.sharding import PartitionSpec as P

MESH = pl.DeviceIdType.MESH
LEVELS = 4
REACH = 2
NEIGH = 5
CAP = 16
STEPS = 6
CHUNK = 4
PIECES = CAP // CHUNK
COPY = 2
SIBLING, NEAR, FAR, PASSED, OWN = range(5)
SPARE = 4
SPAN = 5 * CAP
ZERO = STEPS * SPAN
ROW, PLACE = NEIGH, NEIGH + 1


def window(me, count, level_ref, rows):
    per_line = 128 // rows
    across = lax.broadcasted_iota(jnp.int32, (rows, rows), 1)
    down = lax.broadcasted_iota(jnp.int32, (rows, rows), 0)

    def stand(row):
        return jnp.sum(jnp.where(across == down, row, 0), axis=1, keepdims=True)

    def levels(offset):
        device = jnp.clip(me + offset, 0, count - 1)
        line = level_ref[pl.ds(device // per_line, 1), :]
        part = device % per_line
        here = jnp.zeros((1, rows), jnp.int32)
        for t in range(per_line):
            here = jnp.where(part == t, line[:, t * rows : (t + 1) * rows], here)
        here = jnp.broadcast_to(here, (rows, rows))
        return here, stand(here)

    def ranks(here, column):
        earlier = jnp.where((column == here) & (down < across), 1, 0)
        return jnp.minimum(jnp.sum(earlier, axis=0, keepdims=True), CAP - 1)

    return across, down, stand, levels, ranks


def columns():
    lane = lax.broadcasted_iota(jnp.int32, (1, 128), 1)
    number = lane // CAP
    return lane, number, jnp.where(number < 3, number + 1, 5 - number)


def fill_rows(me, count, level_ref, rows, table_ref):
    across, down, _, levels, ranks = window(me, count, level_ref, rows)
    here, column = levels(0)
    earlier = jnp.where((column == here) & (across < down), 1, 0)
    slot = column * CAP + jnp.sum(earlier, axis=1, keepdims=True)
    lane, _, solves = columns()
    place = slot == jnp.broadcast_to(solves * CAP + lane % CAP, (rows, 128))
    number = lax.broadcasted_iota(jnp.int32, (rows, 128), 0)
    row_of = jnp.sum(jnp.where(place, number, 0), axis=0, keepdims=True)
    table_ref[ROW : ROW + 1, :] = jnp.clip(row_of, 0, rows - 1)
    table_ref[PLACE : PLACE + 1, 0:rows] = jnp.clip(here[0:1, :] * CAP + ranks(here, column), 0, LEVELS * CAP - 1)
    return place


def fill_terms(me, parity, count, level_ref, neighbor_ref, rows, place, table_ref):
    across, _, stand, levels, ranks = window(me, count, level_ref, rows)
    _, number, solves = columns()
    sections = {-2: FAR - parity, -1: PASSED - 3 * parity, 0: OWN, 1: 3 * parity, 2: NEAR + parity}
    codes = []
    for offset in range(-REACH, REACH + 1):
        here, column = levels(offset)
        codes.append(here * 128 + ranks(here, column) + sections[offset] * CAP)
    for k in range(NEIGH):
        row = jnp.broadcast_to(neighbor_ref[k : k + 1, :], (rows, rows))
        which = stand(row) - (me - REACH) * rows
        found = jnp.zeros((rows, rows), jnp.int32)
        for j in range(2 * REACH + 1):
            found += jnp.where(which - j * rows == across, codes[j], 0)
        code = jnp.sum(found, axis=1, keepdims=True)
        by_slot = jnp.sum(jnp.where(place, code, 0), axis=0, keepdims=True)
        spot, level = by_slot & 127, by_slot >> 7
        lower = (number < 3) & (level < solves)
        upper = (number >= 3) & (level > solves)
        index = jnp.where(lower, level * SPAN + spot, jnp.where(upper, (STEPS - level) * SPAN + spot, ZERO))
        table_ref[k : k + 1, :] = jnp.clip(index, 0, ZERO)


def kernel(count, level_hbm, neighbor_hbm, right_hbm, off_hbm, inverse_hbm, out_ref,
           level_ref, neighbor_ref, right, off, inverse, table_v, table, value, solved, leaving, arriving,
           load_sem, send_sem, near_sem, other_sem):
    load_level = pltpu.make_async_copy(level_hbm, level_ref, load_sem.at[4])
    load_level.start()
    me = lax.axis_index("space")
    parity = lax.rem(me, 2)
    sibling = me + 1 - 2 * parity
    to_near, to_far = me - 2 + 4 * parity, me + 2 - 4 * parity
    has_near = (to_near >= 0) & (to_near < count)
    has_far = (to_far >= 0) & (to_far < count)

    near_there, far_there = has_near.astype(jnp.int32), has_far.astype(jnp.int32)
    near_to = sibling + near_there * (to_near - sibling)
    near_at = (SPARE + near_there * (NEAR - SPARE)) * CAP
    far_to = sibling + far_there * (to_far - sibling)
    far_at = (SPARE + far_there * (FAR - SPARE)) * CAP

    barrier = pltpu.get_barrier_semaphore()

    def greet(*targets):
        for target in targets:
            pl.semaphore_signal(barrier, inc=1, device_id={"space": target}, device_id_type=MESH)

    greet(sibling)
    pl.when(has_near)(lambda: greet(to_near))
    pl.when(has_far)(lambda: greet(to_far))

    rows = right.shape[0]
    load_right = pltpu.make_async_copy(right_hbm, right, load_sem.at[0])
    load_right.start()
    load_neighbor = pltpu.make_async_copy(neighbor_hbm, neighbor_ref, load_sem.at[5])
    load_neighbor.start()
    for start in range(0, rows, 4):
        part = pl.ds(start, 4)
        pltpu.make_async_copy(off_hbm.at[part], off.at[part], load_sem.at[1]).start()
    load_off = pltpu.make_async_copy(off_hbm, off, load_sem.at[1])
    load_inverse = pltpu.make_async_copy(inverse_hbm, inverse, load_sem.at[2])
    load_inverse.start()
    load_table = pltpu.make_async_copy(table_v, table, load_sem.at[3])

    table_v[...] = jnp.zeros_like(table_v)
    load_level.wait()
    place = fill_rows(me, count, level_ref, rows, table_v)
    load_table.start()
    solved[ZERO] = jnp.zeros(solved.shape[1:], solved.dtype)

    def remote(source, target, kind, step, to, sem):
        return pltpu.make_async_remote_copy(
            src_ref=source, dst_ref=target, send_sem=send_sem.at[kind, step], recv_sem=sem,
            device_id={"space": to}, device_id_type=MESH,
        )

    def section(step, which, start=0, size=CAP):
        return arriving.at[step, pl.ds(which * CAP + start, size)]

    def own(step, start=0, size=CAP):
        return leaving.at[step, pl.ds(start, size)]

    def send_piece(step, piece):
        for at in range(piece * CHUNK, (piece + 1) * CHUNK, COPY):
            remote(own(step, at, COPY), arriving.at[step, pl.ds(near_at + at, COPY)], 1, step, near_to,
                   near_sem.at[step, near_there * piece + (1 - near_there) * PIECES]).start()
        for at in range(piece * CHUNK, (piece + 1) * CHUNK, COPY):
            remote(own(step, at, COPY), arriving.at[step, pl.ds(far_at + at, COPY)], 2, step, far_to,
                   other_sem.at[step, 3 - 2 * far_there]).start()

    def send_sibling(step):
        remote(own(step), section(step, SIBLING), 0, step, sibling, other_sem.at[step, 0]).start()

    def sent(step):
        def wait(kind):
            there = section(step, SIBLING)
            remote(there, there, kind, step, sibling, near_sem.at[step, 0]).wait_send()

        wait(0)
        wait(1)
        wait(2)
        pl.when(has_far)(lambda: wait(3))

    def arrived(step, which, start, size, sem):
        there = section(step, which, start, size)
        remote(there, there, 0, step, sibling, sem).wait_recv()

    def keep(step, which):
        solved[pl.ds(step * SPAN + which * CAP, CAP)] = arriving[step, pl.ds(which * CAP, CAP)]

    def receive(step):
        @pl.when(has_far)
        def _():
            for piece in range(PIECES):
                at = piece * CHUNK
                arrived(step, NEAR, at, CHUNK, near_sem.at[step, piece])
                remote(section(step, NEAR, at, CHUNK), section(step, PASSED, at, CHUNK), 3, step, sibling,
                       other_sem.at[step, 2]).start()
            keep(step, NEAR)

        @pl.when(jnp.logical_not(has_far))
        def _():
            arrived(step, SPARE, 0, CAP, near_sem.at[step, PIECES])

        @pl.when(jnp.logical_not(has_near))
        def _():
            arrived(step, SPARE, 0, CAP, other_sem.at[step, 3])

        arrived(step, SIBLING, 0, CAP, other_sem.at[step, 0])
        keep(step, SIBLING)

        @pl.when(has_near)
        def _():
            arrived(step, FAR, 0, CAP, other_sem.at[step, 1])
            keep(step, FAR)
            arrived(step, PASSED, 0, CAP, other_sem.at[step, 2])
            keep(step, PASSED)

    def paired(lefts, blocks):
        both = lax.dot_general(
            jnp.concatenate(lefts, axis=0), jnp.concatenate(blocks, axis=0),
            (((1,), (1,)), ((), ())), preferred_element_type=jnp.float32,
        )
        height, width = lefts[0].shape[0], blocks[0].shape[0]
        return both[:height, :width], both[height:, width:]

    def solve(step, level, inverted, leaves):
        def pair(s):
            ats = [(step - 1) * CAP + s + t for t in range(2)]
            two = [table[ROW, at] for at in ats]
            lefts = [jnp.concatenate([solved[table[k, at]] for k in range(NEIGH)], axis=1) for at in ats]
            blocks = [jnp.concatenate([off[row, k] for k in range(NEIGH)], axis=1) for row in two]
            news = [
                (value[level * CAP + s + t].astype(jnp.float32) - total).astype(jnp.bfloat16)
                for t, total in enumerate(paired(lefts, blocks))
            ]
            if inverted:
                news = [new.astype(jnp.bfloat16) for new in paired(news, [inverse[row] for row in two])]
            return news

        everything = []
        for piece in range(PIECES):
            news = sum([pair(piece * CHUNK + t) for t in range(0, CHUNK, 2)], [])
            for t, new in enumerate(news):
                value[level * CAP + piece * CHUNK + t] = new
                if leaves:
                    leaving[step, piece * CHUNK + t] = new
            everything += news
            if leaves:
                send_piece(step, piece)
        if leaves:
            send_sibling(step)
            for t, new in enumerate(everything):
                solved[step * SPAN + OWN * CAP + t] = new
        sent(step - 1)

    def place_values(level, number, first):
        for t in range(CAP):
            here = right[table[ROW, number * CAP + t]]
            value[level * CAP + t] = here
            if first:
                leaving[0, t] = here
                solved[OWN * CAP + t] = here

    load_table.wait()
    load_right.wait()
    place_values(0, 5, True)
    pl.semaphore_wait(barrier, 1 + has_near.astype(jnp.int32) + has_far.astype(jnp.int32))
    for piece in range(PIECES):
        send_piece(0, piece)
    send_sibling(0)
    load_neighbor.wait()
    fill_terms(me, parity, count, level_ref, neighbor_ref, rows, place, table_v)
    load_table.start()
    load_table.wait()
    for level in (1, 2, 3):
        place_values(level, level - 1, False)
    load_off.wait()
    load_inverse.wait()

    def forward_step(step, _):
        receive(step - 1)
        solve(step, step, False, True)
        return 0

    def backward_step(step, _):
        receive(step - 1)
        solve(step, STEPS - step, True, True)
        return 0

    lax.fori_loop(1, 3, forward_step, 0)
    lax.fori_loop(3, STEPS, backward_step, 0)
    receive(STEPS - 1)
    solve(STEPS, 0, True, False)

    for i in range(rows):
        out_ref[i] = value[table[PLACE, i]]


def local(count, right_sides, off_blocks, diag_inv, neighbors, level_of):
    width, blk = right_sides.shape[1:]

    def slots(*sizes):
        return pltpu.VMEM((*sizes, width, blk), jnp.bfloat16)

    return pl.pallas_call(
        functools.partial(kernel, count),
        out_shape=pltpu.VMEM(right_sides.shape, jnp.bfloat16),
        in_specs=[pl.BlockSpec(memory_space=pl.ANY)] * 5,
        out_specs=pl.BlockSpec(memory_space=pltpu.VMEM),
        scratch_shapes=[
            pltpu.VMEM((level_of.shape[0] // 128, 128), jnp.int32),
            pltpu.VMEM(neighbors.shape[::-1], jnp.int32),
            pltpu.VMEM(right_sides.shape, jnp.bfloat16),
            pltpu.VMEM(off_blocks.shape, jnp.bfloat16),
            pltpu.VMEM(diag_inv.shape, jnp.bfloat16),
            pltpu.VMEM((8, 128), jnp.int32),
            pltpu.SMEM((8, 128), jnp.int32),
            slots(LEVELS * CAP),
            slots(STEPS * SPAN + 1),
            slots(STEPS, CAP),
            slots(STEPS, 5 * CAP),
            pltpu.SemaphoreType.DMA((6,)),
            pltpu.SemaphoreType.DMA((4, STEPS)),
            pltpu.SemaphoreType.DMA((STEPS, PIECES + 1)),
            pltpu.SemaphoreType.DMA((STEPS, 4)),
        ],
        compiler_params=pltpu.CompilerParams(
            collective_id=0, has_side_effects=True, vmem_limit_bytes=56 * 1024 * 1024
        ),
        cost_estimate=pl.CostEstimate(flops=600_000_000, bytes_accessed=7_000_000, transcendentals=0),
    )(level_of.reshape(-1, 128), neighbors.T, right_sides, off_blocks, diag_inv)


def solution(mesh):
    in_specs = (
        P("space", "rhs", None),
        P("space", None, None, None),
        P("space", None, None),
        P("space", None),
        P(),
    )
    return jax.shard_map(
        functools.partial(local, mesh.shape["space"]),
        mesh=mesh, in_specs=in_specs, out_specs=P("space", "rhs", None), check_vma=False,
    )
```

```python
import functools

import jax
import jax.numpy as jnp
from jax import lax
from jax.experimental import pallas as pl
from jax.experimental.pallas import tpu as pltpu
from jax.sharding import PartitionSpec as P

MESH = pl.DeviceIdType.MESH
LEVELS = 4
REACH = 2
NEIGH = 5
CAP = 16
STEPS = 6
CHUNK = 4
PIECES = CAP // CHUNK
COPY = 2
SIBLING, NEAR, FAR, PASSED, OWN = range(5)
SPARE = 4
SPAN = 5 * CAP
ZERO = STEPS * SPAN
ROW, PLACE = NEIGH, NEIGH + 1


def window(me, count, level_ref, rows):
    per_line = 128 // rows
    across = lax.broadcasted_iota(jnp.int32, (rows, rows), 1)
    down = lax.broadcasted_iota(jnp.int32, (rows, rows), 0)

    def stand(row):
        return jnp.sum(jnp.where(across == down, row, 0), axis=1, keepdims=True)

    def levels(offset):
        device = jnp.clip(me + offset, 0, count - 1)
        line = level_ref[pl.ds(device // per_line, 1), :]
        part = device % per_line
        here = jnp.zeros((1, rows), jnp.int32)
        for t in range(per_line):
            here = jnp.where(part == t, line[:, t * rows : (t + 1) * rows], here)
        here = jnp.broadcast_to(here, (rows, rows))
        return here, stand(here)

    def ranks(here, column):
        earlier = jnp.where((column == here) & (down < across), 1, 0)
        return jnp.minimum(jnp.sum(earlier, axis=0, keepdims=True), CAP - 1)

    return across, down, stand, levels, ranks


def columns():
    lane = lax.broadcasted_iota(jnp.int32, (1, 128), 1)
    number = lane // CAP
    return lane, number, jnp.where(number < 3, number + 1, 5 - number)


def fill_rows(me, count, level_ref, rows, table_ref):
    across, down, _, levels, ranks = window(me, count, level_ref, rows)
    here, column = levels(0)
    earlier = jnp.where((column == here) & (across < down), 1, 0)
    slot = column * CAP + jnp.sum(earlier, axis=1, keepdims=True)
    lane, _, solves = columns()
    place = slot == jnp.broadcast_to(solves * CAP + lane % CAP, (rows, 128))
    number = lax.broadcasted_iota(jnp.int32, (rows, 128), 0)
    row_of = jnp.sum(jnp.where(place, number, 0), axis=0, keepdims=True)
    table_ref[ROW : ROW + 1, :] = jnp.clip(row_of, 0, rows - 1)
    table_ref[PLACE : PLACE + 1, 0:rows] = jnp.clip(here[0:1, :] * CAP + ranks(here, column), 0, LEVELS * CAP - 1)
    return place


def fill_terms(me, parity, count, level_ref, neighbor_ref, rows, place, table_ref):
    across, _, stand, levels, ranks = window(me, count, level_ref, rows)
    _, number, solves = columns()
    sections = {-2: FAR - parity, -1: PASSED - 3 * parity, 0: OWN, 1: 3 * parity, 2: NEAR + parity}
    codes = []
    for offset in range(-REACH, REACH + 1):
        here, column = levels(offset)
        codes.append(here * 128 + ranks(here, column) + sections[offset] * CAP)
    for k in range(NEIGH):
        row = jnp.broadcast_to(neighbor_ref[k : k + 1, :], (rows, rows))
        which = stand(row) - (me - REACH) * rows
        found = jnp.zeros((rows, rows), jnp.int32)
        for j in range(2 * REACH + 1):
            found += jnp.where(which - j * rows == across, codes[j], 0)
        code = jnp.sum(found, axis=1, keepdims=True)
        by_slot = jnp.sum(jnp.where(place, code, 0), axis=0, keepdims=True)
        spot, level = by_slot & 127, by_slot >> 7
        lower = (number < 3) & (level < solves)
        upper = (number >= 3) & (level > solves)
        index = jnp.where(lower, level * SPAN + spot, jnp.where(upper, (STEPS - level) * SPAN + spot, ZERO))
        table_ref[k : k + 1, :] = jnp.clip(index, 0, ZERO)


def kernel(count, level_hbm, neighbor_hbm, right_hbm, off_hbm, inverse_hbm, out_ref,
           level_ref, neighbor_ref, right, off, inverse, table_v, table, value, solved, leaving, arriving,
           load_sem, send_sem, near_sem, other_sem):
    load_level = pltpu.make_async_copy(level_hbm, level_ref, load_sem.at[4])
    load_level.start()
    me = lax.axis_index("space")
    parity = lax.rem(me, 2)
    sibling = me + 1 - 2 * parity
    to_near, to_far = me - 2 + 4 * parity, me + 2 - 4 * parity
    has_near = (to_near >= 0) & (to_near < count)
    has_far = (to_far >= 0) & (to_far < count)

    near_there, far_there = has_near.astype(jnp.int32), has_far.astype(jnp.int32)
    near_to = sibling + near_there * (to_near - sibling)
    near_at = (SPARE + near_there * (NEAR - SPARE)) * CAP
    far_to = sibling + far_there * (to_far - sibling)
    far_at = (SPARE + far_there * (FAR - SPARE)) * CAP

    barrier = pltpu.get_barrier_semaphore()

    def greet(*targets):
        for target in targets:
            pl.semaphore_signal(barrier, inc=1, device_id={"space": target}, device_id_type=MESH)

    greet(sibling)
    pl.when(has_near)(lambda: greet(to_near))
    pl.when(has_far)(lambda: greet(to_far))

    rows = right.shape[0]
    load_right = pltpu.make_async_copy(right_hbm, right, load_sem.at[0])
    load_right.start()
    load_neighbor = pltpu.make_async_copy(neighbor_hbm, neighbor_ref, load_sem.at[5])
    load_neighbor.start()
    for start in range(0, rows, 4):
        part = pl.ds(start, 4)
        pltpu.make_async_copy(off_hbm.at[part], off.at[part], load_sem.at[1]).start()
    load_off = pltpu.make_async_copy(off_hbm, off, load_sem.at[1])
    load_inverse = pltpu.make_async_copy(inverse_hbm, inverse, load_sem.at[2])
    load_inverse.start()
    load_table = pltpu.make_async_copy(table_v, table, load_sem.at[3])

    table_v[...] = jnp.zeros_like(table_v)
    load_level.wait()
    place = fill_rows(me, count, level_ref, rows, table_v)
    load_table.start()
    solved[ZERO] = jnp.zeros(solved.shape[1:], solved.dtype)

    def remote(source, target, kind, step, to, sem):
        return pltpu.make_async_remote_copy(
            src_ref=source, dst_ref=target, send_sem=send_sem.at[kind, step], recv_sem=sem,
            device_id={"space": to}, device_id_type=MESH,
        )

    def section(step, which, start=0, size=CAP):
        return arriving.at[step, pl.ds(which * CAP + start, size)]

    def own(step, start=0, size=CAP):
        return leaving.at[step, pl.ds(start, size)]

    def send_piece(step, piece):
        for at in range(piece * CHUNK, (piece + 1) * CHUNK, COPY):
            remote(own(step, at, COPY), arriving.at[step, pl.ds(near_at + at, COPY)], 1, step, near_to,
                   near_sem.at[step, near_there * piece + (1 - near_there) * PIECES]).start()
        for at in range(piece * CHUNK, (piece + 1) * CHUNK, COPY):
            remote(own(step, at, COPY), arriving.at[step, pl.ds(far_at + at, COPY)], 2, step, far_to,
                   other_sem.at[step, 3 - 2 * far_there]).start()
        at = piece * CHUNK
        remote(own(step, at, CHUNK), section(step, SIBLING, at, CHUNK), 0, step, sibling,
               other_sem.at[step, 0]).start()

    def sent(step):
        def wait(kind):
            there = section(step, SIBLING)
            remote(there, there, kind, step, sibling, near_sem.at[step, 0]).wait_send()

        wait(0)
        wait(1)
        wait(2)
        pl.when(has_far)(lambda: wait(3))

    def arrived(step, which, start, size, sem):
        there = section(step, which, start, size)
        remote(there, there, 0, step, sibling, sem).wait_recv()

    def keep(step, which):
        solved[pl.ds(step * SPAN + which * CAP, CAP)] = arriving[step, pl.ds(which * CAP, CAP)]

    def receive(step):
        @pl.when(has_far)
        def _():
            for piece in range(PIECES):
                at = piece * CHUNK
                arrived(step, NEAR, at, CHUNK, near_sem.at[step, piece])
                for start in range(at, at + CHUNK, COPY):
                    remote(section(step, NEAR, start, COPY), section(step, PASSED, start, COPY), 3, step, sibling,
                           other_sem.at[step, 2]).start()
            keep(step, NEAR)

        @pl.when(jnp.logical_not(has_far))
        def _():
            arrived(step, SPARE, 0, CAP, near_sem.at[step, PIECES])

        @pl.when(jnp.logical_not(has_near))
        def _():
            arrived(step, SPARE, 0, CAP, other_sem.at[step, 3])

        arrived(step, SIBLING, 0, CAP, other_sem.at[step, 0])
        keep(step, SIBLING)

        @pl.when(has_near)
        def _():
            arrived(step, FAR, 0, CAP, other_sem.at[step, 1])
            keep(step, FAR)
            arrived(step, PASSED, 0, CAP, other_sem.at[step, 2])
            keep(step, PASSED)

    def paired(lefts, blocks):
        both = lax.dot_general(
            jnp.concatenate(lefts, axis=0), jnp.concatenate(blocks, axis=0),
            (((1,), (1,)), ((), ())), preferred_element_type=jnp.float32,
        )
        height, width = lefts[0].shape[0], blocks[0].shape[0]
        return both[:height, :width], both[height:, width:]

    def solve(step, level, inverted, leaves):
        def pair(s):
            ats = [(step - 1) * CAP + s + t for t in range(2)]
            two = [table[ROW, at] for at in ats]
            lefts = [jnp.concatenate([solved[table[k, at]] for k in range(NEIGH)], axis=1) for at in ats]
            blocks = [jnp.concatenate([off[row, k] for k in range(NEIGH)], axis=1) for row in two]
            news = [
                (value[level * CAP + s + t].astype(jnp.float32) - total).astype(jnp.bfloat16)
                for t, total in enumerate(paired(lefts, blocks))
            ]
            if inverted:
                news = [new.astype(jnp.bfloat16) for new in paired(news, [inverse[row] for row in two])]
            return news

        everything = []
        for piece in range(PIECES):
            news = sum([pair(piece * CHUNK + t) for t in range(0, CHUNK, 2)], [])
            for t, new in enumerate(news):
                value[level * CAP + piece * CHUNK + t] = new
                if leaves:
                    leaving[step, piece * CHUNK + t] = new
            everything += news
            if leaves:
                send_piece(step, piece)
        if leaves:
            for t, new in enumerate(everything):
                solved[step * SPAN + OWN * CAP + t] = new
        sent(step - 1)

    def place_values(level, number, first):
        for t in range(CAP):
            here = right[table[ROW, number * CAP + t]]
            value[level * CAP + t] = here
            if first:
                leaving[0, t] = here
                solved[OWN * CAP + t] = here

    load_table.wait()
    load_right.wait()
    place_values(0, 5, True)
    pl.semaphore_wait(barrier, 1 + has_near.astype(jnp.int32) + has_far.astype(jnp.int32))
    for piece in range(PIECES):
        send_piece(0, piece)
    load_neighbor.wait()
    fill_terms(me, parity, count, level_ref, neighbor_ref, rows, place, table_v)
    load_table.start()
    load_table.wait()
    for level in (1, 2, 3):
        place_values(level, level - 1, False)
    load_off.wait()
    load_inverse.wait()

    def forward_step(step, _):
        receive(step - 1)
        solve(step, step, False, True)
        return 0

    def backward_step(step, _):
        receive(step - 1)
        solve(step, STEPS - step, True, True)
        return 0

    lax.fori_loop(1, 3, forward_step, 0)
    lax.fori_loop(3, STEPS, backward_step, 0)
    receive(STEPS - 1)
    solve(STEPS, 0, True, False)

    for i in range(rows):
        out_ref[i] = value[table[PLACE, i]]


def local(count, right_sides, off_blocks, diag_inv, neighbors, level_of):
    width, blk = right_sides.shape[1:]

    def slots(*sizes):
        return pltpu.VMEM((*sizes, width, blk), jnp.bfloat16)

    return pl.pallas_call(
        functools.partial(kernel, count),
        out_shape=pltpu.VMEM(right_sides.shape, jnp.bfloat16),
        in_specs=[pl.BlockSpec(memory_space=pl.ANY)] * 5,
        out_specs=pl.BlockSpec(memory_space=pltpu.VMEM),
        scratch_shapes=[
            pltpu.VMEM((level_of.shape[0] // 128, 128), jnp.int32),
            pltpu.VMEM(neighbors.shape[::-1], jnp.int32),
            pltpu.VMEM(right_sides.shape, jnp.bfloat16),
            pltpu.VMEM(off_blocks.shape, jnp.bfloat16),
            pltpu.VMEM(diag_inv.shape, jnp.bfloat16),
            pltpu.VMEM((8, 128), jnp.int32),
            pltpu.SMEM((8, 128), jnp.int32),
            slots(LEVELS * CAP),
            slots(STEPS * SPAN + 1),
            slots(STEPS, CAP),
            slots(STEPS, 5 * CAP),
            pltpu.SemaphoreType.DMA((6,)),
            pltpu.SemaphoreType.DMA((4, STEPS)),
            pltpu.SemaphoreType.DMA((STEPS, PIECES + 1)),
            pltpu.SemaphoreType.DMA((STEPS, 4)),
        ],
        compiler_params=pltpu.CompilerParams(
            collective_id=0, has_side_effects=True, vmem_limit_bytes=56 * 1024 * 1024
        ),
        cost_estimate=pl.CostEstimate(flops=600_000_000, bytes_accessed=7_000_000, transcendentals=0),
    )(level_of.reshape(-1, 128), neighbors.T, right_sides, off_blocks, diag_inv)


def solution(mesh):
    in_specs = (
        P("space", "rhs", None),
        P("space", None, None, None),
        P("space", None, None),
        P("space", None),
        P(),
    )
    return jax.shard_map(
        functools.partial(local, mesh.shape["space"]),
        mesh=mesh, in_specs=in_specs, out_specs=P("space", "rhs", None), check_vma=False,
    )
```

```python
import functools

import jax
import jax.numpy as jnp
from jax import lax
from jax.experimental import pallas as pl
from jax.experimental.pallas import tpu as pltpu
from jax.sharding import PartitionSpec as P

MESH = pl.DeviceIdType.MESH
LEVELS = 4
REACH = 2
NEIGH = 5
CAP = 16
STEPS = 6
CHUNK = 4
PIECES = CAP // CHUNK
COPY = 1
SIBLING, NEAR, FAR, PASSED, OWN = range(5)
SPARE = 4
SPAN = 5 * CAP
ZERO = STEPS * SPAN
ROW, PLACE = NEIGH, NEIGH + 1


def window(me, count, level_ref, rows):
    per_line = 128 // rows
    across = lax.broadcasted_iota(jnp.int32, (rows, rows), 1)
    down = lax.broadcasted_iota(jnp.int32, (rows, rows), 0)

    def stand(row):
        return jnp.sum(jnp.where(across == down, row, 0), axis=1, keepdims=True)

    def levels(offset):
        device = jnp.clip(me + offset, 0, count - 1)
        line = level_ref[pl.ds(device // per_line, 1), :]
        part = device % per_line
        here = jnp.zeros((1, rows), jnp.int32)
        for t in range(per_line):
            here = jnp.where(part == t, line[:, t * rows : (t + 1) * rows], here)
        here = jnp.broadcast_to(here, (rows, rows))
        return here, stand(here)

    def ranks(here, column):
        earlier = jnp.where((column == here) & (down < across), 1, 0)
        return jnp.minimum(jnp.sum(earlier, axis=0, keepdims=True), CAP - 1)

    return across, down, stand, levels, ranks


def columns():
    lane = lax.broadcasted_iota(jnp.int32, (1, 128), 1)
    number = lane // CAP
    return lane, number, jnp.where(number < 3, number + 1, 5 - number)


def fill_rows(me, count, level_ref, rows, table_ref):
    across, down, _, levels, ranks = window(me, count, level_ref, rows)
    here, column = levels(0)
    earlier = jnp.where((column == here) & (across < down), 1, 0)
    slot = column * CAP + jnp.sum(earlier, axis=1, keepdims=True)
    lane, _, solves = columns()
    place = slot == jnp.broadcast_to(solves * CAP + lane % CAP, (rows, 128))
    number = lax.broadcasted_iota(jnp.int32, (rows, 128), 0)
    row_of = jnp.sum(jnp.where(place, number, 0), axis=0, keepdims=True)
    table_ref[ROW : ROW + 1, :] = jnp.clip(row_of, 0, rows - 1)
    table_ref[PLACE : PLACE + 1, 0:rows] = jnp.clip(here[0:1, :] * CAP + ranks(here, column), 0, LEVELS * CAP - 1)
    return place


def fill_terms(me, parity, count, level_ref, neighbor_ref, rows, place, table_ref):
    across, _, stand, levels, ranks = window(me, count, level_ref, rows)
    _, number, solves = columns()
    sections = {-2: FAR - parity, -1: PASSED - 3 * parity, 0: OWN, 1: 3 * parity, 2: NEAR + parity}
    codes = []
    for offset in range(-REACH, REACH + 1):
        here, column = levels(offset)
        codes.append(here * 128 + ranks(here, column) + sections[offset] * CAP)
    for k in range(NEIGH):
        row = jnp.broadcast_to(neighbor_ref[k : k + 1, :], (rows, rows))
        which = stand(row) - (me - REACH) * rows
        found = jnp.zeros((rows, rows), jnp.int32)
        for j in range(2 * REACH + 1):
            found += jnp.where(which - j * rows == across, codes[j], 0)
        code = jnp.sum(found, axis=1, keepdims=True)
        by_slot = jnp.sum(jnp.where(place, code, 0), axis=0, keepdims=True)
        spot, level = by_slot & 127, by_slot >> 7
        lower = (number < 3) & (level < solves)
        upper = (number >= 3) & (level > solves)
        index = jnp.where(lower, level * SPAN + spot, jnp.where(upper, (STEPS - level) * SPAN + spot, ZERO))
        table_ref[k : k + 1, :] = jnp.clip(index, 0, ZERO)


def kernel(count, level_hbm, neighbor_hbm, right_hbm, off_hbm, inverse_hbm, out_ref,
           level_ref, neighbor_ref, right, off, inverse, table_v, table, value, solved, leaving, arriving,
           load_sem, send_sem, near_sem, other_sem):
    load_level = pltpu.make_async_copy(level_hbm, level_ref, load_sem.at[4])
    load_level.start()
    me = lax.axis_index("space")
    parity = lax.rem(me, 2)
    sibling = me + 1 - 2 * parity
    to_near, to_far = me - 2 + 4 * parity, me + 2 - 4 * parity
    has_near = (to_near >= 0) & (to_near < count)
    has_far = (to_far >= 0) & (to_far < count)

    near_there, far_there = has_near.astype(jnp.int32), has_far.astype(jnp.int32)
    near_to = sibling + near_there * (to_near - sibling)
    near_at = (SPARE + near_there * (NEAR - SPARE)) * CAP
    far_to = sibling + far_there * (to_far - sibling)
    far_at = (SPARE + far_there * (FAR - SPARE)) * CAP

    barrier = pltpu.get_barrier_semaphore()

    def greet(*targets):
        for target in targets:
            pl.semaphore_signal(barrier, inc=1, device_id={"space": target}, device_id_type=MESH)

    greet(sibling)
    pl.when(has_near)(lambda: greet(to_near))
    pl.when(has_far)(lambda: greet(to_far))

    rows = right.shape[0]
    load_right = pltpu.make_async_copy(right_hbm, right, load_sem.at[0])
    load_right.start()
    load_neighbor = pltpu.make_async_copy(neighbor_hbm, neighbor_ref, load_sem.at[5])
    load_neighbor.start()
    for start in range(0, rows, 4):
        part = pl.ds(start, 4)
        pltpu.make_async_copy(off_hbm.at[part], off.at[part], load_sem.at[1]).start()
    load_off = pltpu.make_async_copy(off_hbm, off, load_sem.at[1])
    load_inverse = pltpu.make_async_copy(inverse_hbm, inverse, load_sem.at[2])
    load_inverse.start()
    load_table = pltpu.make_async_copy(table_v, table, load_sem.at[3])

    table_v[...] = jnp.zeros_like(table_v)
    load_level.wait()
    place = fill_rows(me, count, level_ref, rows, table_v)
    load_table.start()
    solved[ZERO] = jnp.zeros(solved.shape[1:], solved.dtype)

    def remote(source, target, kind, step, to, sem):
        return pltpu.make_async_remote_copy(
            src_ref=source, dst_ref=target, send_sem=send_sem.at[kind, step], recv_sem=sem,
            device_id={"space": to}, device_id_type=MESH,
        )

    def section(step, which, start=0, size=CAP):
        return arriving.at[step, pl.ds(which * CAP + start, size)]

    def own(step, start=0, size=CAP):
        return leaving.at[step, pl.ds(start, size)]

    def send_piece(step, piece):
        for at in range(piece * CHUNK, (piece + 1) * CHUNK, COPY):
            remote(own(step, at, COPY), arriving.at[step, pl.ds(near_at + at, COPY)], 1, step, near_to,
                   near_sem.at[step, near_there * piece + (1 - near_there) * PIECES]).start()
        for at in range(piece * CHUNK, (piece + 1) * CHUNK, COPY):
            remote(own(step, at, COPY), arriving.at[step, pl.ds(far_at + at, COPY)], 2, step, far_to,
                   other_sem.at[step, 3 - 2 * far_there]).start()

    def send_sibling(step):
        remote(own(step), section(step, SIBLING), 0, step, sibling, other_sem.at[step, 0]).start()

    def sent(step):
        def wait(kind):
            there = section(step, SIBLING)
            remote(there, there, kind, step, sibling, near_sem.at[step, 0]).wait_send()

        wait(0)
        wait(1)
        wait(2)
        pl.when(has_far)(lambda: wait(3))

    def arrived(step, which, start, size, sem):
        there = section(step, which, start, size)
        remote(there, there, 0, step, sibling, sem).wait_recv()

    def keep(step, which):
        solved[pl.ds(step * SPAN + which * CAP, CAP)] = arriving[step, pl.ds(which * CAP, CAP)]

    def receive(step):
        @pl.when(has_far)
        def _():
            for piece in range(PIECES):
                at = piece * CHUNK
                arrived(step, NEAR, at, CHUNK, near_sem.at[step, piece])
                remote(section(step, NEAR, at, CHUNK), section(step, PASSED, at, CHUNK), 3, step, sibling,
                       other_sem.at[step, 2]).start()
            keep(step, NEAR)

        @pl.when(jnp.logical_not(has_far))
        def _():
            arrived(step, SPARE, 0, CAP, near_sem.at[step, PIECES])

        @pl.when(jnp.logical_not(has_near))
        def _():
            arrived(step, SPARE, 0, CAP, other_sem.at[step, 3])

        arrived(step, SIBLING, 0, CAP, other_sem.at[step, 0])
        keep(step, SIBLING)

        @pl.when(has_near)
        def _():
            arrived(step, FAR, 0, CAP, other_sem.at[step, 1])
            keep(step, FAR)
            arrived(step, PASSED, 0, CAP, other_sem.at[step, 2])
            keep(step, PASSED)

    def paired(lefts, blocks):
        both = lax.dot_general(
            jnp.concatenate(lefts, axis=0), jnp.concatenate(blocks, axis=0),
            (((1,), (1,)), ((), ())), preferred_element_type=jnp.float32,
        )
        height, width = lefts[0].shape[0], blocks[0].shape[0]
        return both[:height, :width], both[height:, width:]

    def solve(step, level, inverted, leaves):
        def pair(s):
            ats = [(step - 1) * CAP + s + t for t in range(2)]
            two = [table[ROW, at] for at in ats]
            lefts = [jnp.concatenate([solved[table[k, at]] for k in range(NEIGH)], axis=1) for at in ats]
            blocks = [jnp.concatenate([off[row, k] for k in range(NEIGH)], axis=1) for row in two]
            news = [
                (value[level * CAP + s + t].astype(jnp.float32) - total).astype(jnp.bfloat16)
                for t, total in enumerate(paired(lefts, blocks))
            ]
            if inverted:
                news = [new.astype(jnp.bfloat16) for new in paired(news, [inverse[row] for row in two])]
            return news

        everything = []
        for piece in range(PIECES):
            news = sum([pair(piece * CHUNK + t) for t in range(0, CHUNK, 2)], [])
            for t, new in enumerate(news):
                value[level * CAP + piece * CHUNK + t] = new
                if leaves:
                    leaving[step, piece * CHUNK + t] = new
            everything += news
            if leaves:
                send_piece(step, piece)
        if leaves:
            send_sibling(step)
            for t, new in enumerate(everything):
                solved[step * SPAN + OWN * CAP + t] = new
        sent(step - 1)

    def place_values(level, number, first):
        for t in range(CAP):
            here = right[table[ROW, number * CAP + t]]
            value[level * CAP + t] = here
            if first:
                leaving[0, t] = here
                solved[OWN * CAP + t] = here

    load_table.wait()
    load_right.wait()
    place_values(0, 5, True)
    pl.semaphore_wait(barrier, 1 + has_near.astype(jnp.int32) + has_far.astype(jnp.int32))
    for piece in range(PIECES):
        send_piece(0, piece)
    send_sibling(0)
    load_neighbor.wait()
    fill_terms(me, parity, count, level_ref, neighbor_ref, rows, place, table_v)
    load_table.start()
    load_table.wait()
    for level in (1, 2, 3):
        place_values(level, level - 1, False)
    load_off.wait()
    load_inverse.wait()

    def forward_step(step, _):
        receive(step - 1)
        solve(step, step, False, True)
        return 0

    def backward_step(step, _):
        receive(step - 1)
        solve(step, STEPS - step, True, True)
        return 0

    lax.fori_loop(1, 3, forward_step, 0)
    lax.fori_loop(3, STEPS, backward_step, 0)
    receive(STEPS - 1)
    solve(STEPS, 0, True, False)

    for i in range(rows):
        out_ref[i] = value[table[PLACE, i]]


def local(count, right_sides, off_blocks, diag_inv, neighbors, level_of):
    width, blk = right_sides.shape[1:]

    def slots(*sizes):
        return pltpu.VMEM((*sizes, width, blk), jnp.bfloat16)

    return pl.pallas_call(
        functools.partial(kernel, count),
        out_shape=pltpu.VMEM(right_sides.shape, jnp.bfloat16),
        in_specs=[pl.BlockSpec(memory_space=pl.ANY)] * 5,
        out_specs=pl.BlockSpec(memory_space=pltpu.VMEM),
        scratch_shapes=[
            pltpu.VMEM((level_of.shape[0] // 128, 128), jnp.int32),
            pltpu.VMEM(neighbors.shape[::-1], jnp.int32),
            pltpu.VMEM(right_sides.shape, jnp.bfloat16),
            pltpu.VMEM(off_blocks.shape, jnp.bfloat16),
            pltpu.VMEM(diag_inv.shape, jnp.bfloat16),
            pltpu.VMEM((8, 128), jnp.int32),
            pltpu.SMEM((8, 128), jnp.int32),
            slots(LEVELS * CAP),
            slots(STEPS * SPAN + 1),
            slots(STEPS, CAP),
            slots(STEPS, 5 * CAP),
            pltpu.SemaphoreType.DMA((6,)),
            pltpu.SemaphoreType.DMA((4, STEPS)),
            pltpu.SemaphoreType.DMA((STEPS, PIECES + 1)),
            pltpu.SemaphoreType.DMA((STEPS, 4)),
        ],
        compiler_params=pltpu.CompilerParams(
            collective_id=0, has_side_effects=True, vmem_limit_bytes=56 * 1024 * 1024
        ),
        cost_estimate=pl.CostEstimate(flops=600_000_000, bytes_accessed=7_000_000, transcendentals=0),
    )(level_of.reshape(-1, 128), neighbors.T, right_sides, off_blocks, diag_inv)


def solution(mesh):
    in_specs = (
        P("space", "rhs", None),
        P("space", None, None, None),
        P("space", None, None),
        P("space", None),
        P(),
    )
    return jax.shard_map(
        functools.partial(local, mesh.shape["space"]),
        mesh=mesh, in_specs=in_specs, out_specs=P("space", "rhs", None), check_vma=False,
    )
```
